256 devices in a mesh: frames: 64 (over x, z, core), mp: 4 (over y).
Axes of the slice: x: 4, y: 4, z: 8, core: 2. Of those that a mesh axis runs over, the one named last changes fastest.
Arguments:
- frames: bfloat16 [1024, 64, 1152], P('frames'), may hold values from -6 to 6
- keyframes: int32 [256, 16], P('frames'), may hold values from 0 to 1023, as said below
- query_states: bfloat16 [256, 32, 768], P('frames'), may hold values from -6 to 6
- w_query: bfloat16 [768, 768], P(None, 'mp'), may hold values from -1 to 1
- w_key: bfloat16 [1152, 768], P(None, 'mp'), may hold values from -1 to 1
- w_value: bfloat16 [1152, 768], P(None, 'mp'), may hold values from -0.1875 to 0.1875
- w_out: bfloat16 [768, 768], P('mp'), may hold values from -0.21875 to 0.21875
- out_grad: bfloat16 [256, 32, 768], P('frames'), may hold values from -6 to 6
Outputs:
- attended: bfloat16 [256, 32, 768], P('frames', None, 'mp')
- query_grad: bfloat16 [256, 32, 768], P('frames', None, 'mp')
- frame_grad: bfloat16 [1024, 64, 1152], P('frames', None, 'mp')
The draws below stay inside these ranges and needn't reach their ends.
Inputs may be any that keep to these rules, and one draw needn't show every extreme that they name: `keyframes`: each entry names a frame. The 64 picks of the questions of one index of frames fall on owners (frame // 16) in groups of exactly 2: every owner gets either 0 or 2 of them.
All inputs are finite; a program needn't handle non-finite values.
Results may differ from the reference program's by a relative error of at most 0.04.
The reference program's roundings to bfloat16 on the way (of `queries`, `weights`, `mixed`, `d_mixed` and `d_scores`) count: a program that leaves them out, or rounds other values in their place, can miss the bound.
Values may be sent and summed in bfloat16 or wider, within the bound.
No kernel may reach another device: no remote copies, remote signals or barrier semaphores. Data moves between devices by JAX's collectives and lax.ppermute only.
A program may use at most 128 MiB of HBM per device.

```python
import jax
import jax.numpy as jnp
from jax import lax

D_FEAT = 1152
HEADS = 12
HEAD_DIM = 64
HID = 768
NQ = 32
TOK = 64
KEYS = 16
QS_DEV = 4
FR_DEV = 16
CAP = 2
FRAMES = 1024
QUESTIONS = 256
N_FRAMES = 64


def shared_projection(key):
    key = jax.random.fold_in(key, 101)
    return jnp.clip(jax.random.normal(key, (HID, HID), jnp.float32), -6.0, 6.0) * HID ** (-0.5)


def draw_keyframes(key, part):
    key = jax.random.fold_in(key, 7)
    first, second, third = jax.random.split(key, 3)
    count = QS_DEV * KEYS
    table = jax.vmap(lambda k: jax.random.permutation(k, N_FRAMES))(jax.random.split(first, N_FRAMES))
    group = jnp.arange(count) // CAP
    owners = table[:, group]
    shuffle = jax.vmap(lambda k: jax.random.permutation(k, count))(jax.random.split(second, N_FRAMES))
    owners = jnp.take_along_axis(owners, shuffle, axis=1)
    local = jax.random.randint(third, (N_FRAMES, count), 0, FR_DEV)
    return (owners * FR_DEV + local).reshape(QUESTIONS, KEYS).astype(jnp.int32)


def draw_w_query(key, part):
    base = shared_projection(key)
    return base.astype(jnp.bfloat16)


def draw_w_key(key, part):
    key = jax.random.fold_in(key, 13)
    noise = jnp.clip(jax.random.normal(key, (D_FEAT, HID), jnp.float32), -6.0, 6.0)
    result = noise * D_FEAT ** (-0.5)
    return result.astype(jnp.bfloat16)


def draw_query_states(key, part):
    key = jax.random.fold_in(key, 17)
    result = jnp.clip(jax.random.normal(key, (QUESTIONS, NQ, HID), jnp.float32), -6.0, 6.0)
    return result.astype(jnp.bfloat16)


def draw_frames(key, part):
    key = jax.random.fold_in(key, 19)
    result = jnp.clip(jax.random.normal(key, (FRAMES, TOK, D_FEAT), jnp.float32), -6.0, 6.0)
    return result.astype(jnp.bfloat16)


def block_scale(own_key, dims, shards, least, largest):
    def one(axis_at, shards_of):
        steps = jax.random.uniform(jax.random.fold_in(jax.random.fold_in(own_key, 6), axis_at), (shards_of,), jnp.float32, least / len(shards), largest / len(shards))
        return jnp.repeat(jnp.exp(steps), dims[axis_at] // shards_of).reshape((-1,) + (1,) * (len(dims) - axis_at - 1))

    level = one(*shards[0])
    for cut in shards[1:]:
        level = level * one(*cut)
    return level


def bell_draw(stream_key, shape, deviation, most, cuts=(), held_as=jnp.bfloat16):
    level = block_scale(stream_key, shape, cuts, -0.22, 0.18) if cuts else 1.0
    drawn = jax.random.normal(stream_key, shape, jnp.float32) * deviation * level
    return jnp.minimum(jnp.maximum(drawn, -most), most).astype(held_as)


def setup_inputs(seed: int = 0) -> dict:
    key_of = jax.random.split(jax.random.key(seed), 9)
    frames = draw_frames(jax.random.fold_in(key_of[8], 71), 0)
    keyframes = draw_keyframes(jax.random.fold_in(key_of[8], 71), 0)
    query_states = draw_query_states(jax.random.fold_in(key_of[8], 71), 0)
    w_query = draw_w_query(jax.random.fold_in(key_of[8], 71), 0)
    w_key = draw_w_key(jax.random.fold_in(key_of[8], 71), 0)
    w_value = bell_draw(key_of[5], (D_FEAT, HID), D_FEAT ** -0.5, 0.1875, ((1, 4),))
    w_out = bell_draw(key_of[6], (HID, HID), HID ** -0.5, 0.21875, ((0, 4),))
    out_grad = bell_draw(key_of[7], (QUESTIONS, NQ, HID), 1.0, 6.0, ((0, 64),))
    return dict(frames=frames, keyframes=keyframes, query_states=query_states, w_query=w_query, w_key=w_key, w_value=w_value, w_out=w_out, out_grad=out_grad)


def reference(frames, keyframes, query_states, w_query, w_key, w_value, w_out, out_grad):
    scale = HEAD_DIM ** -0.5

    def project(block):
        flat = block.reshape(-1, D_FEAT)
        k_part = jnp.dot(flat, w_key, preferred_element_type=jnp.float32).astype(jnp.bfloat16)
        v_part = jnp.dot(flat, w_value, preferred_element_type=jnp.float32).astype(jnp.bfloat16)
        return k_part.reshape(TOK, HID), v_part.reshape(TOK, HID)

    key_bank, value_bank = lax.map(project, frames)

    def question(args):
        picks, states, cotangent = args
        keys = key_bank[picks].reshape(KEYS * TOK, HEADS, HEAD_DIM)
        values = value_bank[picks].reshape(KEYS * TOK, HEADS, HEAD_DIM)
        queries = jnp.dot(states, w_query, preferred_element_type=jnp.float32).astype(jnp.bfloat16)
        queries = queries.reshape(NQ, HEADS, HEAD_DIM)
        scores = jnp.einsum('nhd,khd->hnk', queries.astype(jnp.float32), keys.astype(jnp.float32)) * scale
        probs = jax.nn.softmax(scores, axis=-1)
        weights = probs.astype(jnp.bfloat16)
        mixed = jnp.einsum('hnk,khd->nhd', weights.astype(jnp.float32), values.astype(jnp.float32))
        mixed = mixed.astype(jnp.bfloat16).reshape(NQ, HID)
        attended = jnp.dot(mixed, w_out, preferred_element_type=jnp.float32).astype(jnp.bfloat16)
        d_mixed = jnp.dot(cotangent, w_out.T, preferred_element_type=jnp.float32).astype(jnp.bfloat16)
        d_mixed = d_mixed.reshape(NQ, HEADS, HEAD_DIM)
        d_probs = jnp.einsum('nhd,khd->hnk', d_mixed.astype(jnp.float32), values.astype(jnp.float32))
        d_scores = probs * (d_probs - jnp.sum(probs * d_probs, axis=-1, keepdims=True)) * scale
        d_scores = d_scores.astype(jnp.bfloat16)
        d_queries = jnp.einsum('hnk,khd->nhd', d_scores.astype(jnp.float32), keys.astype(jnp.float32))
        d_queries = d_queries.astype(jnp.bfloat16).reshape(NQ, HID)
        query_grad = jnp.dot(d_queries, w_query.T, preferred_element_type=jnp.float32).astype(jnp.bfloat16)
        d_keys = jnp.einsum('hnk,nhd->khd', d_scores.astype(jnp.float32), queries.astype(jnp.float32)).astype(jnp.bfloat16)
        d_values = jnp.einsum('hnk,nhd->khd', weights.astype(jnp.float32), d_mixed.astype(jnp.float32)).astype(jnp.bfloat16)
        return attended, query_grad, d_keys.reshape(KEYS, TOK, HID), d_values.reshape(KEYS, TOK, HID)

    attended, query_grad, d_keys, d_values = lax.map(question, (keyframes, query_states, out_grad))
    flat_ids = keyframes.reshape(-1).astype(jnp.int32)
    key_sum = jax.ops.segment_sum(d_keys.reshape(-1, TOK, HID).astype(jnp.float32), flat_ids, num_segments=FRAMES)
    value_sum = jax.ops.segment_sum(d_values.reshape(-1, TOK, HID).astype(jnp.float32), flat_ids, num_segments=FRAMES)
    key_sum = key_sum.astype(jnp.bfloat16)
    value_sum = value_sum.astype(jnp.bfloat16)

    def back(args):
        k_block, v_block = args
        grad = jnp.dot(k_block, w_key.T, preferred_element_type=jnp.float32)
        grad = grad + jnp.dot(v_block, w_value.T, preferred_element_type=jnp.float32)
        return grad.astype(jnp.bfloat16)

    frame_grad = lax.map(back, (key_sum, value_sum))
    return attended, query_grad, frame_grad
```

```python
import functools

import jax
import jax.numpy as jnp
from jax import lax
from jax.experimental import pallas as pl
from jax.experimental.pallas import tpu as pltpu
from jax.sharding import PartitionSpec as P

HEAD_DIM = 64
NT = (((1,), (1,)), ((), ()))
TN = (((0,), (0,)), ((), ()))
NN = (((1,), (0,)), ((), ()))
F32 = jnp.float32
BF16 = jnp.bfloat16


def dot(a, b, dims):
    return lax.dot_general(a, b, dims, preferred_element_type=F32)


def head_masks(heads, wide):
    lane = lax.broadcasted_iota(jnp.int32, (1, wide), 1) // HEAD_DIM
    low = [(lane == h).astype(BF16) for h in range(heads)]
    high = [(lane == h + 1).astype(BF16) for h in range(heads)]
    return low, high


def spread(block, masks):
    return jnp.concatenate([block * m for m in masks], axis=0)


def gathered(block, masks, nq):
    total = block[:nq] * masks[0].astype(F32)
    for h in range(1, len(masks)):
        total = total + block[h * nq:(h + 1) * nq] * masks[h].astype(F32)
    return total


def pick_of(code, frames_here):
    code = jnp.maximum(code - 1, 0)
    return code // frames_here, code % frames_here


def products(x_ref, kv_ref, src, code, nq, tok, quests, frames_here, low, high):
    quest, local = pick_of(code, frames_here)
    rows = pl.multiple_of((src * quests + quest) * nq, nq)
    keys = pl.multiple_of(local * tok, tok)
    qm = spread(x_ref[pl.ds(rows, nq), 0:256], low)
    dm = spread(x_ref[pl.ds(rows, nq), 128:384], high)
    k = kv_ref[pl.ds(keys, tok), 0:256]
    v = kv_ref[pl.ds(keys, tok), 128:384]
    return dot(k, qm, NT), dot(v, dm, NT), qm, dm, k, v, keys


def stats_kernel(codes_ref, x_ref, kv_ref, out_ref, *, srcs, cap, nq, tok, quests, frames_here, heads):
    low, high = head_masks(heads, 256)

    def step(src, carry):
        @pl.when(codes_ref[src * cap] > 0)
        def _():
            for r in range(cap):
                s, dp, *_ = products(
                    x_ref, kv_ref, src, codes_ref[src * cap + r], nq, tok, quests, frames_here, low, high
                )
                m = jnp.max(s, axis=0, keepdims=True)
                e = jnp.exp(s - m)
                out_ref[src, 3 * r:3 * r + 1, 0:heads * nq] = m
                out_ref[src, 3 * r + 1:3 * r + 2, 0:heads * nq] = jnp.sum(e, axis=0, keepdims=True)
                out_ref[src, 3 * r + 2:3 * r + 3, 0:heads * nq] = jnp.sum(e * dp, axis=0, keepdims=True)

        return carry

    lax.fori_loop(0, srcs, step, 0)


def combine_kernel(quest_ref, st_ref, out_ref, *, cap, quests):
    ids = [quest_ref[r] for r in range(cap)]
    top = [st_ref[:, 3 * r, :] for r in range(cap)]
    size = [st_ref[:, 3 * r + 1, :] for r in range(cap)]
    mean = [st_ref[:, 3 * r + 2, :] for r in range(cap)]
    outs = [[jnp.zeros_like(top[0]) for _ in range(3)] for _ in range(cap)]
    for j in range(quests):
        on = [ids[r] == j for r in range(cap)]
        big = functools.reduce(
            jnp.maximum,
            [jnp.max(jnp.where(on[r], top[r], -jnp.inf), axis=0, keepdims=True) for r in range(cap)],
        )
        norm, delta = 0.0, 0.0
        for r in range(cap):
            e = jnp.exp(top[r] - big)
            norm = norm + jnp.sum(jnp.where(on[r], e * size[r], 0.0), axis=0, keepdims=True)
            delta = delta + jnp.sum(jnp.where(on[r], e * mean[r], 0.0), axis=0, keepdims=True)
        inv = 1.0 / norm
        for r in range(cap):
            for i, val in enumerate((big, inv, delta * inv)):
                outs[r][i] = jnp.where(on[r], val, outs[r][i])
    for r in range(cap):
        for i in range(3):
            out_ref[:, 3 * r + i, :] = outs[r][i]


def main_kernel(
    codes_ref, x_ref, kv_ref, st_ref, ret_ref, sum_ref, acc_ref, *, srcs, cap, nq, tok, quests, frames_here, heads, scale
):
    low, high = head_masks(heads, 256)
    acc_ref[...] = jnp.zeros_like(acc_ref)
    wide = heads * nq

    def step(src, carry):
        @pl.when(codes_ref[src * cap] > 0)
        def _():
            for r in range(cap):
                s, dp, qm, dm, k, v, keys = products(
                    x_ref, kv_ref, src, codes_ref[src * cap + r], nq, tok, quests, frames_here, low, high
                )
                m = st_ref[src, 3 * r:3 * r + 1, 0:wide]
                inv = st_ref[src, 3 * r + 1:3 * r + 2, 0:wide]
                delta = st_ref[src, 3 * r + 2:3 * r + 3, 0:wide]
                p = jnp.exp(s - m) * inv
                w = p.astype(BF16)
                ds = (p * (dp - delta)).astype(BF16)
                o = gathered(dot(w, v, TN), high, nq)
                dq = gathered(dot(ds, k, TN), low, nq) * scale
                dk = dot(ds, qm, NN)
                dv = dot(w, dm, NN)
                row = pl.multiple_of((src * cap + r) * nq, nq)
                ret_ref[pl.ds(row, nq), 0:128] = dq[:, 0:128].astype(BF16)
                ret_ref[pl.ds(row, nq), 128:256] = (dq[:, 128:256] + o[:, 0:128]).astype(BF16)
                ret_ref[pl.ds(row, nq), 256:384] = o[:, 128:256].astype(BF16)
                acc_ref[pl.ds(keys, tok), 0:128] += dk[:, 0:128]
                acc_ref[pl.ds(keys, tok), 128:256] += dk[:, 128:256] + dv[:, 0:128]
                acc_ref[pl.ds(keys, tok), 256:384] += dv[:, 128:256]

        @pl.when(codes_ref[src * cap] == 0)
        def _():
            row = pl.multiple_of(src * cap * nq, nq)
            ret_ref[pl.ds(row, cap * nq), :] = jnp.zeros((cap * nq, ret_ref.shape[1]), BF16)

        return carry

    lax.fori_loop(0, srcs, step, 0)
    sum_ref[...] = acc_ref[...].astype(BF16)


def collect_kernel(codes_ref, ret_ref, out_ref, acc_ref, *, slots, nq, frames_here):
    acc_ref[...] = jnp.zeros_like(acc_ref)

    def step(slot, carry):
        code = codes_ref[slot]

        @pl.when(code > 0)
        def _():
            quest, _ = pick_of(code, frames_here)
            to = pl.multiple_of(quest * nq, nq)
            at = pl.multiple_of(slot * nq, nq)
            acc_ref[pl.ds(to, nq), :] += ret_ref[pl.ds(at, nq), :].astype(F32)

        return carry

    lax.fori_loop(0, slots, step, 0)
    out_ref[...] = acc_ref[...].astype(BF16)


def call(kernel, out_shape, ins, scratch=()):
    spaces = {"s": pltpu.SMEM, "v": pltpu.VMEM}
    return pl.pallas_call(
        kernel,
        out_shape=out_shape,
        in_specs=[pl.BlockSpec(memory_space=spaces[i]) for i in ins],
        out_specs=jax.tree.map(lambda _: pl.BlockSpec(memory_space=pltpu.VMEM), out_shape),
        scratch_shapes=list(scratch),
        compiler_params=pltpu.CompilerParams(vmem_limit_bytes=40 * 1024 * 1024),
    )


def body(frames, keyframes, query_states, w_query, w_key, w_value, w_out, out_grad):
    owners = lax.axis_size("frames")
    shards = lax.axis_size("mp")
    fr_count, tok, width = frames.shape
    quests, keys = keyframes.shape
    nq = query_states.shape[1]
    hid = query_states.shape[2]
    cols = w_key.shape[1]
    heads = cols // HEAD_DIM
    scale = HEAD_DIM ** (-0.5)
    count = quests * keys
    cap = max(2, count // owners)

    picks = keyframes.reshape(-1)
    owner = picks // fr_count
    position = jnp.arange(count)
    same = owner[:, None] == owner[None, :]
    rank = jnp.sum(jnp.logical_and(same, position[None, :] < position[:, None]), axis=1)
    code = picks % fr_count + fr_count * (position // keys) + 1
    slot = owner * cap + rank
    requests = jnp.sum(
        jnp.where(slot[None, :] == jnp.arange(owners * cap)[:, None], code[None, :], 0), axis=1
    ).astype(jnp.int32)
    incoming = lax.all_to_all(
        requests.reshape(owners, cap), "frames", split_axis=0, concat_axis=0, tiled=True
    ).reshape(-1)
    quest_of = jnp.where(requests > 0, (requests - 1) // fr_count, -1).reshape(owners, cap)
    quest_of = jnp.broadcast_to(quest_of.T[:, :, None], (cap, owners, 128))

    queries = jnp.dot(query_states.reshape(quests * nq, hid), w_query, preferred_element_type=F32)
    d_mixed = lax.dot_general(out_grad.reshape(quests * nq, hid), w_out, NT, preferred_element_type=F32)
    local = jnp.concatenate([queries.astype(BF16) * scale, d_mixed.astype(BF16)], axis=1)
    everyone = lax.all_gather(local, "frames", axis=0, tiled=True)

    w_both = jnp.concatenate([w_key, w_value], axis=1)
    bank = jnp.dot(frames.reshape(fr_count * tok, width), w_both, preferred_element_type=F32).astype(BF16)
    w_mine = lax.all_to_all(
        jnp.concatenate(
            [w_query.reshape(shards, hid // shards, cols), w_out.reshape(cols, shards, hid // shards).swapaxes(0, 1)],
            axis=2,
        ),
        "mp",
        split_axis=0,
        concat_axis=0,
        tiled=True,
    )

    dims = dict(srcs=owners, cap=cap, nq=nq, tok=tok, quests=quests, frames_here=fr_count, heads=heads)
    stat_shape = jax.ShapeDtypeStruct((owners, 8, 128), F32)
    stats = call(functools.partial(stats_kernel, **dims), stat_shape, "svv")(incoming, everyone, bank)
    stats = lax.all_to_all(stats, "frames", split_axis=0, concat_axis=0, tiled=True)
    stats = call(functools.partial(combine_kernel, cap=cap, quests=quests), stat_shape, "vv")(quest_of, stats)
    stats = lax.all_to_all(stats, "frames", split_axis=0, concat_axis=0, tiled=True)
    partial, sums = call(
        functools.partial(main_kernel, scale=scale, **dims),
        (
            jax.ShapeDtypeStruct((owners * cap * nq, 2 * cols), BF16),
            jax.ShapeDtypeStruct((fr_count * tok, 2 * cols), BF16),
        ),
        "svvv",
        [pltpu.VMEM((fr_count * tok, 2 * cols), F32)],
    )(incoming, everyone, bank, stats)
    partial = lax.all_to_all(
        partial.reshape(owners, cap * nq, 2 * cols), "frames", split_axis=0, concat_axis=0, tiled=True
    ).reshape(owners * cap * nq, 2 * cols)

    grad_terms = lax.dot_general(w_both, sums, NT, preferred_element_type=F32).astype(BF16)
    frame_grad = lax.psum_scatter(grad_terms, "mp", scatter_dimension=0, tiled=True)
    frame_grad = frame_grad.T.reshape(fr_count, tok, width // shards)

    mine = call(
        functools.partial(collect_kernel, slots=owners * cap, nq=nq, frames_here=fr_count),
        jax.ShapeDtypeStruct((quests * nq, 2 * cols), BF16),
        "sv",
        [pltpu.VMEM((quests * nq, 2 * cols), F32)],
    )(requests, partial)
    full = lax.all_gather(mine, "mp", axis=0)
    query_grad = jnp.einsum("jrh,jch->rc", full[:, :, :cols], w_mine[:, :, :cols], preferred_element_type=F32)
    attended = jnp.einsum("jrh,jhc->rc", full[:, :, cols:], w_mine[:, :, cols:], preferred_element_type=F32)
    return (
        attended.astype(BF16).reshape(quests, nq, hid // shards),
        query_grad.astype(BF16).reshape(quests, nq, hid // shards),
        frame_grad,
    )


def solution(mesh):
    placed = (
        P("frames", None, None),
        P("frames", None),
        P("frames", None, None),
        P(None, "mp"),
        P(None, "mp"),
        P(None, "mp"),
        P("mp", None),
        P("frames", None, None),
    )
    return jax.shard_map(
        body,
        mesh=mesh,
        in_specs=placed,
        out_specs=(P("frames", None, "mp"), P("frames", None, "mp"), P("frames", None, "mp")),
        check_vma=False,
    )
```

```python
import functools

import jax
import jax.numpy as jnp
from jax import lax
from jax.experimental import pallas as pl
from jax.experimental.pallas import tpu as pltpu
from jax.sharding import PartitionSpec as P

HEAD_DIM = 64
NT = (((1,), (1,)), ((), ()))
TN = (((0,), (0,)), ((), ()))
NN = (((1,), (0,)), ((), ()))
F32 = jnp.float32
BF16 = jnp.bfloat16


def dot(a, b, dims):
    return lax.dot_general(a, b, dims, preferred_element_type=F32)


def head_masks(heads, wide):
    lane = lax.broadcasted_iota(jnp.int32, (1, wide), 1) // HEAD_DIM
    low = [(lane == h).astype(BF16) for h in range(heads)]
    high = [(lane == h + 1).astype(BF16) for h in range(heads)]
    return low, high


def spread(block, masks):
    return jnp.concatenate([block * m for m in masks], axis=0)


def gathered(block, masks, nq):
    total = block[:nq] * masks[0].astype(F32)
    for h in range(1, len(masks)):
        total = total + block[h * nq:(h + 1) * nq] * masks[h].astype(F32)
    return total


AXES = (4, 8, 2)
FIRST = 3


def frames_perm(dx=0, dz=0, dc=0):
    nx, nz, nc = AXES
    pairs = []
    for x in range(nx):
        for z in range(nz):
            for c in range(nc):
                to = (((x + dx) % nx) * nz + (z + dz) % nz) * nc + (c + dc) % nc
                pairs.append(((x * nz + z) * nc + c, to))
    return pairs


def planes():
    nx, nz, nc = AXES
    number = lambda x, z, c: (x * nz + z) * nc + c
    flat = [[number(x, z, c) for x in range(nx) for c in range(nc)] for z in range(nz)]
    line = [[number(x, z, c) for z in range(nz)] for x in range(nx) for c in range(nc)]
    return flat, line


def hop(value, **shift):
    return lax.ppermute(value, "frames", frames_perm(**shift))


def plan_kernel(codes_ref, me_ref, order_ref, size_ref, at_ref, *, cap, quests, nq, tok, frames_here):
    nx, nz, nc = AXES
    owners = nx * nz * nc
    bits = frames_here.bit_length() - 1
    me = me_ref[0]
    x, z, c = lax.div(me, nz * nc), lax.rem(lax.div(me, nc), nz), lax.rem(me, nc)

    def step(block, found):
        at, core, across = lax.div(block, nc * nx), lax.rem(lax.div(block, nx), nc), lax.rem(block, nx)
        away = jnp.where(lax.rem(at, 2) == 1, lax.div(at + 1, 2), nz - lax.div(at, 2))
        there = lax.rem(x - across + nx, nx) * nz + lax.rem(z - away + nz, nz)
        src = there * nc + lax.rem(c + core, nc)
        asks = (lax.rem(there, nz) * nx + lax.div(there, nz)) * nc + lax.rem(c + core, nc)
        valid = codes_ref[asks * cap] > 0
        order_ref[jnp.where(valid, found, owners - 1 - (block - found))] = src
        for r in range(cap):
            code = jnp.maximum(codes_ref[asks * cap + r] - 1, 0)
            row = (block * quests + (code >> bits)) * nq
            at_ref[src * cap + r] = jnp.where(valid, row, 0)
            at_ref[(owners + src) * cap + r] = (code & (frames_here - 1)) * tok
        return found + jnp.where(valid, 1, 0)

    near = lax.fori_loop(0, FIRST * nx * nc, step, 0)
    size_ref[1] = near
    size_ref[0] = lax.fori_loop(FIRST * nx * nc, owners, step, near)


def load_rows(pieces, x_ref, sems):
    copies, row = [], 0
    full = pieces[0].shape[0]
    for i, piece in enumerate(pieces):
        size = piece.shape[0]
        if size == full:
            row = i * full
        else:
            half, core = divmod(i - (len(pieces) - 4), 2)
            row = (len(pieces) - 4 + core) * full + half * size
        copies.append(pltpu.make_async_copy(piece, x_ref.at[pl.ds(row, size)], sems.at[i]))
        copies[-1].start()
    return copies


def in_groups(order_ref, size_ref, copies, group, step):
    early = size_ref[1] // group
    for c in copies[:2 * FIRST]:
        c.wait()
    lax.fori_loop(0, early, step, 0)
    for c in copies[2 * FIRST:]:
        c.wait()
    last = (size_ref[0] + group - 1) // group
    lax.fori_loop(early, last, step, 0)
    return last


def group_of(i, group, cap, order_ref):
    srcs = [order_ref[i * group + g] for g in range(group)]
    return srcs, [src * cap + r for src in srcs for r in range(cap)]


def rows_of(at_ref, slots, x_ref, kv_ref, nq, tok, low, high):
    at = [pl.multiple_of(at_ref[slot], nq) for slot in slots]
    keys = [pl.multiple_of(at_ref[at_ref.shape[0] // 2 + slot], tok) for slot in slots]
    qm = [spread(x_ref[pl.ds(a, nq), 0:256], low) for a in at]
    dm = [spread(x_ref[pl.ds(a, nq), 128:384], high) for a in at]
    k = [kv_ref[pl.ds(a, tok), 0:256] for a in keys]
    v = [kv_ref[pl.ds(a, tok), 128:384] for a in keys]
    s = [dot(a, b, NT) for a, b in zip(k, qm)]
    dp = [dot(a, b, NT) for a, b in zip(v, dm)]
    return s, dp, qm, dm, k, v, keys


def stats_kernel(order_ref, size_ref, at_ref, kv_ref, *refs, cap, nq, tok, heads, group):
    *pieces, out_ref, x_ref, sems = refs
    low, high = head_masks(heads, 256)
    copies = load_rows(pieces, x_ref, sems)
    wide = heads * nq

    def step(i, carry):
        srcs, slots = group_of(i, group, cap, order_ref)
        s, dp, *_ = rows_of(at_ref, slots, x_ref, kv_ref, nq, tok, low, high)
        m = [jnp.max(a, axis=0, keepdims=True) for a in s]
        e = [jnp.exp(a - b) for a, b in zip(s, m)]
        for n, (a, b, c) in enumerate(zip(m, e, dp)):
            src, r = srcs[n // cap], 3 * (n % cap)
            out_ref[src, r:r + 1, 0:wide] = a
            out_ref[src, r + 1:r + 2, 0:wide] = jnp.sum(b, axis=0, keepdims=True)
            out_ref[src, r + 2:r + 3, 0:wide] = jnp.sum(b * c, axis=0, keepdims=True)
        return carry

    in_groups(order_ref, size_ref, copies, group, step)


def combine_kernel(quest_ref, st_ref, out_ref, *, cap, quests):
    ids = [quest_ref[r] for r in range(cap)]
    top = [st_ref[:, 3 * r, :] for r in range(cap)]
    size = [st_ref[:, 3 * r + 1, :] for r in range(cap)]
    mean = [st_ref[:, 3 * r + 2, :] for r in range(cap)]
    none = jnp.zeros_like(top[0])
    outs = [[none + 3e38, none, none] for _ in range(cap)]
    for j in range(quests):
        on = [ids[r] == j for r in range(cap)]
        big = functools.reduce(
            jnp.maximum,
            [jnp.max(jnp.where(on[r], top[r], -jnp.inf), axis=0, keepdims=True) for r in range(cap)],
        )
        norm, delta = 0.0, 0.0
        for r in range(cap):
            e = jnp.exp(top[r] - big)
            norm = norm + jnp.sum(jnp.where(on[r], e * size[r], 0.0), axis=0, keepdims=True)
            delta = delta + jnp.sum(jnp.where(on[r], e * mean[r], 0.0), axis=0, keepdims=True)
        inv = 1.0 / norm
        for r in range(cap):
            for i, val in enumerate((big, inv, delta * inv)):
                outs[r][i] = jnp.where(on[r], val, outs[r][i])
    for r in range(cap):
        for i in range(3):
            out_ref[:, 3 * r + i, :] = outs[r][i]


def main_kernel(
    order_ref, size_ref, at_ref, kv_ref, st_ref, x_ref, ret_ref, sum_ref, acc_ref, held_ref, sent,
    *, cap, nq, tok, heads, group, scale
):
    low, high = head_masks(heads, 256)
    acc_ref[...] = jnp.zeros_like(acc_ref)
    wide = heads * nq
    size = cap * nq

    def send(src):
        at = pl.ds(pl.multiple_of(src * size, size), size)
        pltpu.make_async_copy(held_ref.at[at], ret_ref.at[at], sent).start()

    def step(i, carry):
        srcs, slots = group_of(i, group, cap, order_ref)
        s, dp, qm, dm, k, v, keys = rows_of(at_ref, slots, x_ref, kv_ref, nq, tok, low, high)
        st = [
            [st_ref[src, 3 * r + n:3 * r + n + 1, 0:wide] for n in range(3)] for src in srcs for r in range(cap)
        ]
        p = [jnp.exp(a - b[0]) * b[1] for a, b in zip(s, st)]
        w = [a.astype(BF16) for a in p]
        ds = [(a * (b - c[2])).astype(BF16) for a, b, c in zip(p, dp, st)]
        o = [gathered(dot(a, b, TN), high, nq) for a, b in zip(w, v)]
        dq = [gathered(dot(a, b, TN), low, nq) * scale for a, b in zip(ds, k)]
        dk = [dot(a, b, NN) for a, b in zip(ds, qm)]
        dv = [dot(a, b, NN) for a, b in zip(w, dm)]
        for n, slot in enumerate(slots):
            row = pl.ds(pl.multiple_of(slot * nq, nq), nq)
            held_ref[row, 0:128] = dq[n][:, 0:128].astype(BF16)
            held_ref[row, 128:256] = (dq[n][:, 128:256] + o[n][:, 0:128]).astype(BF16)
            held_ref[row, 256:384] = o[n][:, 128:256].astype(BF16)
            at = pl.ds(keys[n], tok)
            acc_ref[at, 0:128] += dk[n][:, 0:128]
            acc_ref[at, 128:256] += dk[n][:, 128:256] + dv[n][:, 0:128]
            acc_ref[at, 256:384] += dv[n][:, 128:256]
        for src in srcs:
            send(src)
        return carry

    last = (size_ref[0] + group - 1) // group
    lax.fori_loop(0, last, step, 0)

    def rest(i, carry):
        src = order_ref[i]
        held_ref[pl.ds(pl.multiple_of(src * size, size), size), :] = jnp.zeros((size, held_ref.shape[1]), BF16)
        send(src)
        return carry

    lax.fori_loop(last * group, order_ref.shape[0], rest, 0)
    sum_ref[...] = acc_ref[...].astype(BF16)
    pltpu.make_async_copy(held_ref, ret_ref, sent).wait()


def finish_kernel(*refs, cols):
    *ins, att_ref, grad_ref = refs
    many = len(ins) // 2
    lane = lax.broadcasted_iota(jnp.int32, (1, 256), 1)
    low = (lane < cols).astype(BF16)
    high = (lane >= cols - 128).astype(BF16)
    att, grad = 0.0, 0.0
    for x_ref, w_ref in zip(ins[:many], ins[many:]):
        grad = grad + dot(x_ref[:, 0:256] * low, w_ref[:, 0:256], NT)
        att = att + dot(x_ref[:, 128:384] * high, w_ref[:, 128:384], NT)
    att_ref[...] = att.astype(BF16)
    grad_ref[...] = grad.astype(BF16)


def call(kernel, out_shape, ins, outs, scratch=(), mib=1):
    spaces = {"s": pltpu.SMEM, "v": pltpu.VMEM, "a": pltpu.HBM}
    out_specs = [pl.BlockSpec(memory_space=spaces[i]) for i in outs]
    return pl.pallas_call(
        kernel,
        out_shape=out_shape,
        in_specs=[pl.BlockSpec(memory_space=spaces[i]) for i in ins],
        out_specs=out_specs if len(outs) > 1 else out_specs[0],
        scratch_shapes=list(scratch),
        compiler_params=pltpu.CompilerParams(vmem_limit_bytes=mib * 1024 * 1024),
    )


def mp_hop(value, s):
    many = lax.axis_size("mp")
    return lax.ppermute(value, "mp", [(i, (i + s) % many) for i in range(many)])


def body(frames, keyframes, query_states, w_query, w_key, w_value, w_out, out_grad):
    owners = lax.axis_size("frames")
    shards = lax.axis_size("mp")
    me, shard = lax.axis_index("frames"), lax.axis_index("mp")
    fr_count, tok, width = frames.shape
    quests, keys = keyframes.shape
    nq = query_states.shape[1]
    hid = query_states.shape[2]
    cols = w_key.shape[1]
    heads = cols // HEAD_DIM
    scale = HEAD_DIM ** (-0.5)
    count = quests * keys
    cap = max(2, count // owners)
    group = 4

    queries = jnp.dot(query_states.reshape(quests * nq, hid), w_query, preferred_element_type=F32)
    d_mixed = lax.dot_general(out_grad.reshape(quests * nq, hid), w_out, NT, preferred_element_type=F32)
    local = jnp.concatenate([queries.astype(BF16) * scale, d_mixed.astype(BF16)], axis=1)
    picks = keyframes.reshape(-1)
    owner = picks >> (fr_count.bit_length() - 1)
    position = jnp.arange(count)
    same = owner[:, None] == owner[None, :]
    rank = jnp.sum(jnp.logical_and(same, position[None, :] < position[:, None]), axis=1)
    code = (picks & (fr_count - 1)) + fr_count * (position // keys) + 1
    slot = owner * cap + rank
    requests = jnp.sum(
        jnp.where(slot[None, :] == jnp.arange(owners * cap)[:, None], code[None, :], 0), axis=1
    ).astype(jnp.int32)
    asked = jnp.where(requests > 0, (requests - 1) >> (fr_count.bit_length() - 1), -1)
    quest_of = jnp.broadcast_to(asked.reshape(owners, cap).T[:, :, None], (cap, owners, 128))
    put = jnp.arange(quests * nq)[:, None]
    take = jnp.arange(owners * cap * nq)[None, :]
    pick_sum = jnp.logical_and(put // nq == jnp.repeat(asked, nq)[None, :], put % nq == take % nq).astype(BF16)

    w_both = jnp.concatenate([w_key, w_value], axis=1)
    bank = jnp.dot(frames.reshape(fr_count * tok, width), w_both, preferred_element_type=F32).astype(BF16)
    flat, line = planes()
    nx, nz, nc = AXES
    mine = jnp.concatenate([local] + [hop(local, dx=s) for s in range(1, nx)], axis=0)
    passed = requests.reshape(nx, nz, nc, cap).swapaxes(0, 1).reshape(nz, nx * nc * cap)
    passed = lax.all_to_all(passed, "frames", 0, 0, axis_index_groups=line, tiled=True)
    mine, passed, bank = lax.optimization_barrier((mine, passed, bank))
    incoming = passed.reshape(nz, nx * nc, cap).swapaxes(0, 1).reshape(nx * nc, nz * cap)
    incoming = lax.all_to_all(incoming, "frames", 0, 0, axis_index_groups=flat, tiled=True)
    incoming = incoming.reshape(nx * nc, nz, cap).swapaxes(0, 1).reshape(-1)
    ways = [(mine, mine)]
    ways.append((hop(ways[-1][0], dz=1), hop(ways[-1][1], dz=-1)))
    ways[-1], incoming = lax.optimization_barrier((ways[-1], incoming))
    ints = lambda *shape: jax.ShapeDtypeStruct(shape, jnp.int32)
    order, sizes, at = call(
        functools.partial(plan_kernel, cap=cap, quests=quests, nq=nq, tok=tok, frames_here=fr_count),
        (ints(owners), ints(2), ints(2 * owners * cap)),
        "ss",
        "sss",
    )(incoming, me.astype(jnp.int32).reshape(1))
    ways.append((hop(ways[-1][0], dz=1), hop(ways[-1][1], dz=-1)))
    ways[-1], order, sizes, at, quest_of = lax.optimization_barrier((ways[-1], order, sizes, at, quest_of))
    ways.append((hop(ways[-1][0], dz=1), hop(ways[-1][1], dz=-1)))
    half = mine.shape[0] // 2
    pieces = [mine] + [way for pair in ways[1:] for way in pair]
    pieces += [hop(ways[-1][0][:half], dz=1), hop(ways[-1][1][half:], dz=-1)]
    pieces = [p for piece in pieces for p in (piece, hop(piece, dc=1))]

    dims = dict(cap=cap, nq=nq, tok=tok, heads=heads, group=group)
    held = (owners * cap * nq, 2 * cols)
    stat_shape = jax.ShapeDtypeStruct((owners, 8, 128), F32)
    rows = jax.ShapeDtypeStruct((owners * quests * nq, 2 * cols), BF16)
    stats, rows = call(
        functools.partial(stats_kernel, **dims),
        (stat_shape, rows),
        "sssv" + "a" * len(pieces),
        "vv",
        [pltpu.SemaphoreType.DMA((len(pieces),))],
        4,
    )(order, sizes, at, bank, *pieces)
    stats = lax.all_to_all(stats, "frames", split_axis=0, concat_axis=0, tiled=True)
    stats = call(functools.partial(combine_kernel, cap=cap, quests=quests), stat_shape, "vv", "v")(quest_of, stats)
    stats = lax.all_to_all(stats, "frames", split_axis=0, concat_axis=0, tiled=True)
    partial, sums = call(
        functools.partial(main_kernel, scale=scale, **dims),
        (jax.ShapeDtypeStruct(held, BF16), jax.ShapeDtypeStruct((fr_count * tok, 2 * cols), BF16)),
        "sssvvv",
        "av",
        [
            pltpu.VMEM((fr_count * tok, 2 * cols), F32),
            pltpu.VMEM(held, BF16),
            pltpu.SemaphoreType.DMA(()),
        ],
        10,
    )(order, sizes, at, bank, stats, rows)
    partial = lax.all_to_all(
        partial.reshape(owners, cap * nq, 2 * cols), "frames", split_axis=0, concat_axis=0, tiled=True
    ).reshape(held)

    w_q_out = jnp.concatenate([w_query, w_out.T], axis=1)
    own = [(shard + s) % shards for s in range(shards)]
    part = hid // shards
    w_mine = [lax.dynamic_slice_in_dim(w_q_out, own[s] * part, part, 0) for s in range(shards)]
    w_mine = [w_mine[0]] + [mp_hop(w_mine[s], s) for s in range(1, shards)]
    slab = width // shards
    terms = [
        lax.dot_general(
            sums, lax.dynamic_slice_in_dim(w_both, own[s] * slab, slab, 0), NT, preferred_element_type=F32
        )
        for s in range(shards)
    ]
    frame_grad = terms[0]
    for s in range(1, shards):
        frame_grad = frame_grad + mp_hop(terms[s].astype(BF16), s).astype(F32)

    frame_grad = frame_grad.astype(BF16).reshape(fr_count, tok, slab)
    tied = (partial, frame_grad, w_mine, pick_sum)
    partial, frame_grad, w_mine, pick_sum = lax.optimization_barrier(tied)
    mine = jnp.dot(pick_sum, partial, preferred_element_type=F32).astype(BF16)
    full = [mine] + [mp_hop(mine, s) for s in range(1, shards)]
    out = jax.ShapeDtypeStruct((quests * nq, part), BF16)
    attended, query_grad = call(
        functools.partial(finish_kernel, cols=cols), (out, out), "v" * 2 * shards, "vv", mib=4
    )(*full, *w_mine)
    return (
        attended.reshape(quests, nq, part),
        query_grad.reshape(quests, nq, part),
        frame_grad,
    )


def solution(mesh):
    placed = (
        P("frames", None, None),
        P("frames", None),
        P("frames", None, None),
        P(None, "mp"),
        P(None, "mp"),
        P(None, "mp"),
        P("mp", None),
        P("frames", None, None),
    )
    return jax.shard_map(
        body,
        mesh=mesh,
        in_specs=placed,
        out_specs=(P("frames", None, "mp"), P("frames", None, "mp"), P("frames", None, "mp")),
        check_vma=False,
    )
```

```python
import functools

import jax
import jax.numpy as jnp
from jax import lax
from jax.experimental import pallas as pl
from jax.experimental.pallas import tpu as pltpu
from jax.sharding import PartitionSpec as P

HEAD_DIM = 64
NT = (((1,), (1,)), ((), ()))
TN = (((0,), (0,)), ((), ()))
NN = (((1,), (0,)), ((), ()))
F32 = jnp.float32
BF16 = jnp.bfloat16


def dot(a, b, dims):
    return lax.dot_general(a, b, dims, preferred_element_type=F32)


def head_masks(heads, wide):
    lane = lax.broadcasted_iota(jnp.int32, (1, wide), 1) // HEAD_DIM
    low = [(lane == h).astype(BF16) for h in range(heads)]
    high = [(lane == h + 1).astype(BF16) for h in range(heads)]
    return low, high


def spread(block, masks):
    return jnp.concatenate([block * m for m in masks], axis=0)


def gathered(block, masks, nq):
    total = block[:nq] * masks[0].astype(F32)
    for h in range(1, len(masks)):
        total = total + block[h * nq:(h + 1) * nq] * masks[h].astype(F32)
    return total


AXES = (4, 8, 2)
FIRST = 3


def frames_perm(dx=0, dz=0, dc=0):
    nx, nz, nc = AXES
    pairs = []
    for x in range(nx):
        for z in range(nz):
            for c in range(nc):
                to = (((x + dx) % nx) * nz + (z + dz) % nz) * nc + (c + dc) % nc
                pairs.append(((x * nz + z) * nc + c, to))
    return pairs


def planes():
    nx, nz, nc = AXES
    number = lambda x, z, c: (x * nz + z) * nc + c
    flat = [[number(x, z, c) for x in range(nx) for c in range(nc)] for z in range(nz)]
    line = [[number(x, z, c) for z in range(nz)] for x in range(nx) for c in range(nc)]
    return flat, line


def hop(value, **shift):
    return lax.ppermute(value, "frames", frames_perm(**shift))


def plan_kernel(codes_ref, me_ref, order_ref, size_ref, at_ref, *, cap, quests, nq, tok, frames_here):
    nx, nz, nc = AXES
    owners = nx * nz * nc
    bits = frames_here.bit_length() - 1
    me = me_ref[0]
    x, z, c = lax.div(me, nz * nc), lax.rem(lax.div(me, nc), nz), lax.rem(me, nc)

    def step(block, found):
        at, core, across = lax.div(block, nc * nx), lax.rem(lax.div(block, nx), nc), lax.rem(block, nx)
        away = jnp.where(lax.rem(at, 2) == 1, lax.div(at + 1, 2), nz - lax.div(at, 2))
        there = lax.rem(x - across + nx, nx) * nz + lax.rem(z - away + nz, nz)
        src = there * nc + lax.rem(c + core, nc)
        asks = (lax.rem(there, nz) * nx + across) * nc + core
        valid = codes_ref[asks * cap] > 0
        order_ref[jnp.where(valid, found, owners - 1 - (block - found))] = src
        for r in range(cap):
            code = jnp.maximum(codes_ref[asks * cap + r] - 1, 0)
            row = (block * quests + (code >> bits)) * nq
            at_ref[src * cap + r] = jnp.where(valid, row, 0)
            at_ref[(owners + src) * cap + r] = (code & (frames_here - 1)) * tok
        return found + jnp.where(valid, 1, 0)

    near = lax.fori_loop(0, FIRST * nx * nc, step, 0)
    size_ref[1] = near
    size_ref[0] = lax.fori_loop(FIRST * nx * nc, owners, step, near)


def load_rows(pieces, x_ref, sems):
    copies, row = [], 0
    full = pieces[0].shape[0]
    for i, piece in enumerate(pieces):
        size = piece.shape[0]
        if size == full:
            row = i * full
        else:
            half, core = divmod(i - (len(pieces) - 4), 2)
            row = (len(pieces) - 4 + core) * full + half * size
        copies.append(pltpu.make_async_copy(piece, x_ref.at[pl.ds(row, size)], sems.at[i]))
        copies[-1].start()
    return copies


def in_groups(order_ref, size_ref, copies, group, step):
    early = size_ref[1] // group
    for c in copies[:2 * FIRST]:
        c.wait()
    lax.fori_loop(0, early, step, 0)
    for c in copies[2 * FIRST:]:
        c.wait()
    last = (size_ref[0] + group - 1) // group
    lax.fori_loop(early, last, step, 0)
    return last


def group_of(i, group, cap, order_ref):
    srcs = [order_ref[i * group + g] for g in range(group)]
    return srcs, [src * cap + r for src in srcs for r in range(cap)]


def rows_of(at_ref, slots, x_ref, kv_ref, nq, tok, low, high):
    at = [pl.multiple_of(at_ref[slot], nq) for slot in slots]
    keys = [pl.multiple_of(at_ref[at_ref.shape[0] // 2 + slot], tok) for slot in slots]
    qm = [spread(x_ref[pl.ds(a, nq), 0:256], low) for a in at]
    dm = [spread(x_ref[pl.ds(a, nq), 128:384], high) for a in at]
    k = [kv_ref[pl.ds(a, tok), 0:256] for a in keys]
    v = [kv_ref[pl.ds(a, tok), 128:384] for a in keys]
    s = [dot(a, b, NT) for a, b in zip(k, qm)]
    dp = [dot(a, b, NT) for a, b in zip(v, dm)]
    return s, dp, qm, dm, k, v, keys


def stats_kernel(order_ref, size_ref, at_ref, kv_ref, *refs, cap, nq, tok, heads, group):
    *pieces, out_ref, x_ref, sems = refs
    low, high = head_masks(heads, 256)
    copies = load_rows(pieces, x_ref, sems)
    wide = heads * nq

    def step(i, carry):
        srcs, slots = group_of(i, group, cap, order_ref)
        s, dp, *_ = rows_of(at_ref, slots, x_ref, kv_ref, nq, tok, low, high)
        m = [jnp.max(a, axis=0, keepdims=True) for a in s]
        e = [jnp.exp(a - b) for a, b in zip(s, m)]
        for n, (a, b, c) in enumerate(zip(m, e, dp)):
            src, r = srcs[n // cap], 3 * (n % cap)
            out_ref[src, r:r + 1, 0:wide] = a
            out_ref[src, r + 1:r + 2, 0:wide] = jnp.sum(b, axis=0, keepdims=True)
            out_ref[src, r + 2:r + 3, 0:wide] = jnp.sum(b * c, axis=0, keepdims=True)
        return carry

    in_groups(order_ref, size_ref, copies, group, step)


def combine_kernel(quest_ref, st_ref, out_ref, *, cap, quests):
    ids = [quest_ref[r] for r in range(cap)]
    top = [st_ref[:, 3 * r, :] for r in range(cap)]
    size = [st_ref[:, 3 * r + 1, :] for r in range(cap)]
    mean = [st_ref[:, 3 * r + 2, :] for r in range(cap)]
    none = jnp.zeros_like(top[0])
    outs = [[none + 3e38, none, none] for _ in range(cap)]
    for j in range(quests):
        on = [ids[r] == j for r in range(cap)]
        big = functools.reduce(
            jnp.maximum,
            [jnp.max(jnp.where(on[r], top[r], -jnp.inf), axis=0, keepdims=True) for r in range(cap)],
        )
        norm, delta = 0.0, 0.0
        for r in range(cap):
            e = jnp.exp(top[r] - big)
            norm = norm + jnp.sum(jnp.where(on[r], e * size[r], 0.0), axis=0, keepdims=True)
            delta = delta + jnp.sum(jnp.where(on[r], e * mean[r], 0.0), axis=0, keepdims=True)
        inv = 1.0 / norm
        for r in range(cap):
            for i, val in enumerate((big, inv, delta * inv)):
                outs[r][i] = jnp.where(on[r], val, outs[r][i])
    for r in range(cap):
        for i in range(3):
            out_ref[:, 3 * r + i, :] = outs[r][i]


def main_kernel(
    order_ref, size_ref, at_ref, kv_ref, st_ref, x_ref, ret_ref, sum_ref, acc_ref,
    *, cap, nq, tok, heads, group, scale
):
    low, high = head_masks(heads, 256)
    acc_ref[...] = jnp.zeros_like(acc_ref)
    wide = heads * nq
    size = cap * nq

    nx, nz, nc = AXES

    def place(src):
        column = lax.div(src, nz * nc) * nc + lax.rem(src, nc)
        return pl.multiple_of((column * nz + lax.rem(lax.div(src, nc), nz)) * size, size)

    def step(i, carry):
        srcs, slots = group_of(i, group, cap, order_ref)
        s, dp, qm, dm, k, v, keys = rows_of(at_ref, slots, x_ref, kv_ref, nq, tok, low, high)
        st = [
            [st_ref[src, 3 * r + n:3 * r + n + 1, 0:wide] for n in range(3)] for src in srcs for r in range(cap)
        ]
        p = [jnp.exp(a - b[0]) * b[1] for a, b in zip(s, st)]
        w = [a.astype(BF16) for a in p]
        ds = [(a * (b - c[2])).astype(BF16) for a, b, c in zip(p, dp, st)]
        o = [gathered(dot(a, b, TN), high, nq) for a, b in zip(w, v)]
        dq = [gathered(dot(a, b, TN), low, nq) * scale for a, b in zip(ds, k)]
        dk = [dot(a, b, NN) for a, b in zip(ds, qm)]
        dv = [dot(a, b, NN) for a, b in zip(w, dm)]
        for n in range(len(slots)):
            row = pl.ds(pl.multiple_of(place(srcs[n // cap]) + n % cap * nq, nq), nq)
            ret_ref[row, 0:128] = dq[n][:, 0:128].astype(BF16)
            ret_ref[row, 128:256] = (dq[n][:, 128:256] + o[n][:, 0:128]).astype(BF16)
            ret_ref[row, 256:384] = o[n][:, 128:256].astype(BF16)
            at = pl.ds(keys[n], tok)
            acc_ref[at, 0:128] += dk[n][:, 0:128]
            acc_ref[at, 128:256] += dk[n][:, 128:256] + dv[n][:, 0:128]
            acc_ref[at, 256:384] += dv[n][:, 128:256]
        return carry

    last = (size_ref[0] + group - 1) // group
    lax.fori_loop(0, last, step, 0)

    def rest(i, carry):
        src = order_ref[i]
        ret_ref[pl.ds(place(src), size), :] = jnp.zeros((size, ret_ref.shape[1]), BF16)
        return carry

    lax.fori_loop(last * group, order_ref.shape[0], rest, 0)
    sum_ref[...] = acc_ref[...].astype(BF16)


def merge_kernel(me_ref, pick_ref, ret_ref, *out_refs):
    nz = len(out_refs)
    for s, out_ref in enumerate(out_refs):
        to = lax.rem(me_ref[0] + s, nz)
        rows = jnp.concatenate([ret_ref[u, to] for u in range(ret_ref.shape[0])], axis=0)
        out_ref[...] = dot(pick_ref[to], rows, NN).astype(BF16)


def project_kernel(shard_ref, x_ref, w_ref, *out_refs, cols):
    lane = lax.broadcasted_iota(jnp.int32, (1, 256), 1)
    grad = x_ref[:, 0:256] * (lane < cols).astype(BF16)
    mixed = x_ref[:, 128:384] * (lane >= cols - 128).astype(BF16)
    rows = x_ref.shape[0]
    many = len(out_refs)
    part = w_ref.shape[0] // many
    for s, out_ref in enumerate(out_refs):
        at = pl.ds(pl.multiple_of(lax.rem(shard_ref[0] + s, many) * part, part), part)
        out_ref[0:rows, :] = dot(mixed, w_ref[at, 128:384], NT).astype(out_ref.dtype)
        out_ref[rows:2 * rows, :] = dot(grad, w_ref[at, 0:256], NT).astype(out_ref.dtype)


def call(kernel, out_shape, ins, outs, scratch=(), mib=1):
    spaces = {"s": pltpu.SMEM, "v": pltpu.VMEM, "a": pltpu.HBM}
    out_specs = [pl.BlockSpec(memory_space=spaces[i]) for i in outs]
    return pl.pallas_call(
        kernel,
        out_shape=out_shape,
        in_specs=[pl.BlockSpec(memory_space=spaces[i]) for i in ins],
        out_specs=out_specs if len(outs) > 1 else out_specs[0],
        scratch_shapes=list(scratch),
        compiler_params=pltpu.CompilerParams(vmem_limit_bytes=mib * 1024 * 1024),
    )


def mp_hop(value, s):
    many = lax.axis_size("mp")
    return lax.ppermute(value, "mp", [(i, (i + s) % many) for i in range(many)])


def body(frames, keyframes, query_states, w_query, w_key, w_value, w_out, out_grad):
    owners = lax.axis_size("frames")
    shards = lax.axis_size("mp")
    me, shard = lax.axis_index("frames"), lax.axis_index("mp")
    fr_count, tok, width = frames.shape
    quests, keys = keyframes.shape
    nq = query_states.shape[1]
    hid = query_states.shape[2]
    cols = w_key.shape[1]
    heads = cols // HEAD_DIM
    scale = HEAD_DIM ** (-0.5)
    count = quests * keys
    cap = max(2, count // owners)
    group = 4

    queries = jnp.dot(query_states.reshape(quests * nq, hid), w_query, preferred_element_type=F32)
    d_mixed = lax.dot_general(out_grad.reshape(quests * nq, hid), w_out, NT, preferred_element_type=F32)
    local = jnp.concatenate([queries.astype(BF16) * scale, d_mixed.astype(BF16)], axis=1)
    picks = keyframes.reshape(-1)
    owner = picks >> (fr_count.bit_length() - 1)
    position = jnp.arange(count)
    same = owner[:, None] == owner[None, :]
    rank = jnp.sum(jnp.logical_and(same, position[None, :] < position[:, None]), axis=1)
    code = (picks & (fr_count - 1)) + fr_count * (position // keys) + 1
    slot = owner * cap + rank
    requests = jnp.sum(
        jnp.where(slot[None, :] == jnp.arange(owners * cap)[:, None], code[None, :], 0), axis=1
    ).astype(jnp.int32)
    asked = jnp.where(requests > 0, (requests - 1) >> (fr_count.bit_length() - 1), -1)
    quest_of = jnp.broadcast_to(asked.reshape(owners, cap).T[:, :, None], (cap, owners, 128))

    nx, nz, nc = AXES
    owners = nx * nz * nc
    bits = frames_here.bit_length() - 1
    me = me_ref[0]
    x, z, c = lax.div(me, nz * nc), lax.rem(lax.div(me, nc), nz), lax.rem(me, nc)

    def step(block, found):
        at, core, across = lax.div(block, nc * nx), lax.rem(lax.div(block, nx), nc), lax.rem(block, nx)
        away = jnp.where(lax.rem(at, 2) == 1, lax.div(at + 1, 2), nz - lax.div(at, 2))
        there = lax.rem(x - across + nx, nx) * nz + lax.rem(z - away + nz, nz)
        src = there * nc + lax.rem(c + core, nc)
        asks = (lax.rem(there, nz) * nx + across) * nc + core
        valid = codes_ref[asks * cap] > 0
        order_ref[jnp.where(valid, found, owners - 1 - (block - found))] = src
        for r in range(cap):
            code = jnp.maximum(codes_ref[asks * cap + r] - 1, 0)
            row = (block * quests + (code >> bits)) * nq
            at_ref[src * cap + r] = jnp.where(valid, row, 0)
            at_ref[(owners + src) * cap + r] = (code & (frames_here - 1)) * tok
        return found + jnp.where(valid, 1, 0)

    near = lax.fori_loop(0, FIRST * nx * nc, step, 0)
    size_ref[1] = near
    size_ref[0] = lax.fori_loop(FIRST * nx * nc, owners, step, near)


def load_rows(pieces, x_ref, sems):
    copies, row = [], 0
    full = pieces[0].shape[0]
    for i, piece in enumerate(pieces):
        size = piece.shape[0]
        if size == full:
            row = i * full
        else:
            half, core = divmod(i - (len(pieces) - 4), 2)
            row = (len(pieces) - 4 + core) * full + half * size
        copies.append(pltpu.make_async_copy(piece, x_ref.at[pl.ds(row, size)], sems.at[i]))
        copies[-1].start()
    return copies


def in_groups(order_ref, size_ref, copies, group, step):
    early = size_ref[1] // group
    for c in copies[:2 * FIRST]:
        c.wait()
    lax.fori_loop(0, early, step, 0)
    for c in copies[2 * FIRST:]:
        c.wait()
    last = (size_ref[0] + group - 1) // group
    lax.fori_loop(early, last, step, 0)
    return last


def group_of(i, group, cap, order_ref):
    srcs = [order_ref[i * group + g] for g in range(group)]
    return srcs, [src * cap + r for src in srcs for r in range(cap)]


def rows_of(at_ref, slots, x_ref, kv_ref, nq, tok, low, high):
    at = [pl.multiple_of(at_ref[slot], nq) for slot in slots]
    keys = [pl.multiple_of(at_ref[at_ref.shape[0] // 2 + slot], tok) for slot in slots]
    qm = [spread(x_ref[pl.ds(a, nq), 0:256], low) for a in at]
    dm = [spread(x_ref[pl.ds(a, nq), 128:384], high) for a in at]
    k = [kv_ref[pl.ds(a, tok), 0:256] for a in keys]
    v = [kv_ref[pl.ds(a, tok), 128:384] for a in keys]
    s = [dot(a, b, NT) for a, b in zip(k, qm)]
    dp = [dot(a, b, NT) for a, b in zip(v, dm)]
    return s, dp, qm, dm, k, v, keys


def stats_kernel(order_ref, size_ref, at_ref, kv_ref, *refs, cap, nq, tok, heads, group):
    *pieces, out_ref, x_ref, sems = refs
    low, high = head_masks(heads, 256)
    copies = load_rows(pieces, x_ref, sems)
    wide = heads * nq

    def step(i, carry):
        srcs, slots = group_of(i, group, cap, order_ref)
        s, dp, *_ = rows_of(at_ref, slots, x_ref, kv_ref, nq, tok, low, high)
        m = [jnp.max(a, axis=0, keepdims=True) for a in s]
        e = [jnp.exp(a - b) for a, b in zip(s, m)]
        for n, (a, b, c) in enumerate(zip(m, e, dp)):
            src, r = srcs[n // cap], 3 * (n % cap)
            out_ref[src, r:r + 1, 0:wide] = a
            out_ref[src, r + 1:r + 2, 0:wide] = jnp.sum(b, axis=0, keepdims=True)
            out_ref[src, r + 2:r + 3, 0:wide] = jnp.sum(b * c, axis=0, keepdims=True)
        return carry

    in_groups(order_ref, size_ref, copies, group, step)


def combine_kernel(quest_ref, st_ref, out_ref, *, cap, quests):
    ids = [quest_ref[r] for r in range(cap)]
    top = [st_ref[:, 3 * r, :] for r in range(cap)]
    size = [st_ref[:, 3 * r + 1, :] for r in range(cap)]
    mean = [st_ref[:, 3 * r + 2, :] for r in range(cap)]
    none = jnp.zeros_like(top[0])
    outs = [[none + 3e38, none, none] for _ in range(cap)]
    for j in range(quests):
        on = [ids[r] == j for r in range(cap)]
        big = functools.reduce(
            jnp.maximum,
            [jnp.max(jnp.where(on[r], top[r], -jnp.inf), axis=0, keepdims=True) for r in range(cap)],
        )
        norm, delta = 0.0, 0.0
        for r in range(cap):
            e = jnp.exp(top[r] - big)
            norm = norm + jnp.sum(jnp.where(on[r], e * size[r], 0.0), axis=0, keepdims=True)
            delta = delta + jnp.sum(jnp.where(on[r], e * mean[r], 0.0), axis=0, keepdims=True)
        inv = 1.0 / norm
        for r in range(cap):
            for i, val in enumerate((big, inv, delta * inv)):
                outs[r][i] = jnp.where(on[r], val, outs[r][i])
    for r in range(cap):
        for i in range(3):
            out_ref[:, 3 * r + i, :] = outs[r][i]


def main_kernel(
    order_ref, size_ref, at_ref, kv_ref, st_ref, x_ref, ret_ref, sum_ref, acc_ref,
    *, cap, nq, tok, heads, group, scale
):
    low, high = head_masks(heads, 256)
    acc_ref[...] = jnp.zeros_like(acc_ref)
    wide = heads * nq
    size = cap * nq

    nx, nz, nc = AXES

    def place(src):
        column = lax.div(src, nz * nc) * nc + lax.rem(src, nc)
        return pl.multiple_of((column * nz + lax.rem(lax.div(src, nc), nz)) * size, size)

    def step(i, carry):
        srcs, slots = group_of(i, group, cap, order_ref)
        s, dp, qm, dm, k, v, keys = rows_of(at_ref, slots, x_ref, kv_ref, nq, tok, low, high)
        st = [
            [st_ref[src, 3 * r + n:3 * r + n + 1, 0:wide] for n in range(3)] for src in srcs for r in range(cap)
        ]
        p = [jnp.exp(a - b[0]) * b[1] for a, b in zip(s, st)]
        w = [a.astype(BF16) for a in p]
        ds = [(a * (b - c[2])).astype(BF16) for a, b, c in zip(p, dp, st)]
        o = [gathered(dot(a, b, TN), high, nq) for a, b in zip(w, v)]
        dq = [gathered(dot(a, b, TN), low, nq) * scale for a, b in zip(ds, k)]
        dk = [dot(a, b, NN) for a, b in zip(ds, qm)]
        dv = [dot(a, b, NN) for a, b in zip(w, dm)]
        for n in range(len(slots)):
            row = pl.ds(pl.multiple_of(place(srcs[n // cap]) + n % cap * nq, nq), nq)
            ret_ref[row, 0:128] = dq[n][:, 0:128].astype(BF16)
            ret_ref[row, 128:256] = (dq[n][:, 128:256] + o[n][:, 0:128]).astype(BF16)
            ret_ref[row, 256:384] = o[n][:, 128:256].astype(BF16)
            at = pl.ds(keys[n], tok)
            acc_ref[at, 0:128] += dk[n][:, 0:128]
            acc_ref[at, 128:256] += dk[n][:, 128:256] + dv[n][:, 0:128]
            acc_ref[at, 256:384] += dv[n][:, 128:256]
        return carry

    last = (size_ref[0] + group - 1) // group
    lax.fori_loop(0, last, step, 0)

    def rest(i, carry):
        src = order_ref[i]
        ret_ref[pl.ds(place(src), size), :] = jnp.zeros((size, ret_ref.shape[1]), BF16)
        return carry

    lax.fori_loop(last * group, order_ref.shape[0], rest, 0)
    sum_ref[...] = acc_ref[...].astype(BF16)


def merge_kernel(me_ref, pick_ref, ret_ref, *out_refs):
    nz = len(out_refs)
    for s, out_ref in enumerate(out_refs):
        to = lax.rem(me_ref[0] + s, nz)
        rows = jnp.concatenate([ret_ref[u, to] for u in range(ret_ref.shape[0])], axis=0)
        out_ref[...] = dot(pick_ref[to], rows, NN).astype(BF16)


def finish_kernel(*refs, cols):
    *ins, att_ref, grad_ref = refs
    many = len(ins) // 2
    lane = lax.broadcasted_iota(jnp.int32, (1, 256), 1)
    low = (lane < cols).astype(BF16)
    high = (lane >= cols - 128).astype(BF16)
    att, grad = 0.0, 0.0
    for x_ref, w_ref in zip(ins[:many], ins[many:]):
        grad = grad + dot(x_ref[:, 0:256] * low, w_ref[:, 0:256], NT)
        att = att + dot(x_ref[:, 128:384] * high, w_ref[:, 128:384], NT)
    att_ref[...] = att.astype(BF16)
    grad_ref[...] = grad.astype(BF16)


def call(kernel, out_shape, ins, outs, scratch=(), mib=1):
    spaces = {"s": pltpu.SMEM, "v": pltpu.VMEM, "a": pltpu.HBM}
    out_specs = [pl.BlockSpec(memory_space=spaces[i]) for i in outs]
    return pl.pallas_call(
        kernel,
        out_shape=out_shape,
        in_specs=[pl.BlockSpec(memory_space=spaces[i]) for i in ins],
        out_specs=out_specs if len(outs) > 1 else out_specs[0],
        scratch_shapes=list(scratch),
        compiler_params=pltpu.CompilerParams(vmem_limit_bytes=mib * 1024 * 1024),
    )


def mp_hop(value, s):
    many = lax.axis_size("mp")
    return lax.ppermute(value, "mp", [(i, (i + s) % many) for i in range(many)])


def body(frames, keyframes, query_states, w_query, w_key, w_value, w_out, out_grad):
    owners = lax.axis_size("frames")
    shards = lax.axis_size("mp")
    me, shard = lax.axis_index("frames"), lax.axis_index("mp")
    fr_count, tok, width = frames.shape
    quests, keys = keyframes.shape
    nq = query_states.shape[1]
    hid = query_states.shape[2]
    cols = w_key.shape[1]
    heads = cols // HEAD_DIM
    scale = HEAD_DIM ** (-0.5)
    count = quests * keys
    cap = max(2, count // owners)
    group = 4

    queries = jnp.dot(query_states.reshape(quests * nq, hid), w_query, preferred_element_type=F32)
    d_mixed = lax.dot_general(out_grad.reshape(quests * nq, hid), w_out, NT, preferred_element_type=F32)
    local = jnp.concatenate([queries.astype(BF16) * scale, d_mixed.astype(BF16)], axis=1)
    picks = keyframes.reshape(-1)
    owner = picks >> (fr_count.bit_length() - 1)
    position = jnp.arange(count)
    same = owner[:, None] == owner[None, :]
    rank = jnp.sum(jnp.logical_and(same, position[None, :] < position[:, None]), axis=1)
    code = (picks & (fr_count - 1)) + fr_count * (position // keys) + 1
    slot = owner * cap + rank
    requests = jnp.sum(
        jnp.where(slot[None, :] == jnp.arange(owners * cap)[:, None], code[None, :], 0), axis=1
    ).astype(jnp.int32)
    asked = jnp.where(requests > 0, (requests - 1) >> (fr_count.bit_length() - 1), -1)
    quest_of = jnp.broadcast_to(asked.reshape(owners, cap).T[:, :, None], (cap, owners, 128))
    put = jnp.arange(quests * nq)[:, None]
    take = jnp.arange(owners * cap * nq)[None, :]
    pick_sum = jnp.logical_and(put // nq == jnp.repeat(asked, nq)[None, :], put % nq == take % nq).astype(BF16)

    w_both = jnp.concatenate([w_key, w_value], axis=1)
    bank = jnp.dot(frames.reshape(fr_count * tok, width), w_both, preferred_element_type=F32).astype(BF16)
    flat, line = planes()
    nx, nz, nc = AXES
    mine = jnp.concatenate([local] + [hop(local, dx=s) for s in range(1, nx)], axis=0)
    plane = requests.reshape(nx, nz, nc, cap).swapaxes(0, 1).reshape(1, owners * cap)
    plane = jnp.concatenate([plane, hop(plane, dc=1)], axis=0)
    plane = jnp.concatenate([plane] + [hop(plane, dx=s) for s in range(1, nx)], axis=0)
    mine, plane, bank = lax.optimization_barrier((mine, plane, bank))
    plane = plane.reshape(nx * nc, nz, nx * nc * cap).swapaxes(0, 1).reshape(nz, nx * nc * nx * nc * cap)
    asked = lax.all_to_all(plane, "frames", 0, 0, axis_index_groups=line, tiled=True)
    ways = [(mine, mine)]
    ways.append((hop(ways[-1][0], dz=1), hop(ways[-1][1], dz=-1)))
    ways[-1], asked = lax.optimization_barrier((ways[-1], asked))
    asked = asked.reshape(nz, nx * nc, nx * nc, cap)
    passed = asked[:, 0].reshape(nz, nx * nc * cap)
    column = me // (nz * nc) * nc + me % nc
    incoming = lax.dynamic_index_in_dim(asked, column, 2, keepdims=False).reshape(-1)
    ints = lambda *shape: jax.ShapeDtypeStruct(shape, jnp.int32)
    order, sizes, at = call(
        functools.partial(plan_kernel, cap=cap, quests=quests, nq=nq, tok=tok, frames_here=fr_count),
        (ints(owners), ints(2), ints(2 * owners * cap)),
        "ss",
        "sss",
    )(incoming, me.astype(jnp.int32).reshape(1))
    ways.append((hop(ways[-1][0], dz=1), hop(ways[-1][1], dz=-1)))
    ways[-1], order, sizes, at, quest_of = lax.optimization_barrier((ways[-1], order, sizes, at, quest_of))
    ways.append((hop(ways[-1][0], dz=1), hop(ways[-1][1], dz=-1)))
    half = mine.shape[0] // 2
    pieces = [mine] + [way for pair in ways[1:] for way in pair]
    pieces += [hop(ways[-1][0][:half], dz=1), hop(ways[-1][1][half:], dz=-1)]
    pieces = [p for piece in pieces for p in (piece, hop(piece, dc=1))]

    dims = dict(cap=cap, nq=nq, tok=tok, heads=heads, group=group)
    held = (owners * cap * nq, 2 * cols)
    stat_shape = jax.ShapeDtypeStruct((owners, 8, 128), F32)
    rows = jax.ShapeDtypeStruct((owners * quests * nq, 2 * cols), BF16)
    stats, rows = call(
        functools.partial(stats_kernel, **dims),
        (stat_shape, rows),
        "sssv" + "a" * len(pieces),
        "vv",
        [pltpu.SemaphoreType.DMA((len(pieces),))],
        4,
    )(order, sizes, at, bank, *pieces)
    stats = lax.all_to_all(stats, "frames", split_axis=0, concat_axis=0, tiled=True)
    stats = call(functools.partial(combine_kernel, cap=cap, quests=quests), stat_shape, "vv", "v")(quest_of, stats)
    stats = lax.all_to_all(stats, "frames", split_axis=0, concat_axis=0, tiled=True)
    partial, sums = call(
        functools.partial(main_kernel, scale=scale, **dims),
        (jax.ShapeDtypeStruct(held, BF16), jax.ShapeDtypeStruct((fr_count * tok, 2 * cols), BF16)),
        "sssvvv",
        "vv",
        [pltpu.VMEM((fr_count * tok, 2 * cols), F32)],
        8,
    )(order, sizes, at, bank, stats, rows)
    partial = lax.all_to_all(
        partial.reshape(nx * nc, nz * cap * nq, 2 * cols), "frames", 0, 0, axis_index_groups=flat, tiled=True
    ).reshape(nx * nc, nz, cap * nq, 2 * cols)
    asked = jnp.where(passed > 0, (passed - 1) >> (fr_count.bit_length() - 1), -1)
    put = jnp.arange(quests * nq)[None, :, None]
    take = jnp.arange(nx * nc * cap * nq)[None, None, :]
    asked = jnp.repeat(asked.reshape(nz, 1, nx * nc * cap), nq, axis=2)
    pick_sum = jnp.logical_and(put // nq == asked, put % nq == take % nq).astype(BF16)

    w_q_out = jnp.concatenate([w_query, w_out.T], axis=1)
    own = [(shard + s) % shards for s in range(shards)]
    part = hid // shards
    slab = width // shards
    terms = [
        lax.dot_general(
            sums, lax.dynamic_slice_in_dim(w_both, own[s] * slab, slab, 0), NT, preferred_element_type=F32
        )
        for s in range(shards)
    ]
    frame_grad = terms[0]
    for s in range(1, shards):
        frame_grad = frame_grad + mp_hop(terms[s].astype(BF16), s).astype(F32)

    frame_grad = frame_grad.astype(BF16).reshape(fr_count, tok, slab)
    partial, w_q_out, pick_sum = lax.optimization_barrier((partial, w_q_out, pick_sum))
    mine_shape = jax.ShapeDtypeStruct((quests * nq, 2 * cols), BF16)
    merged = call(merge_kernel, (mine_shape,) * nz, "svv", "v" * nz, mib=4)(
        lax.rem(lax.div(me, nc), nz).astype(jnp.int32).reshape(1), pick_sum, partial
    )
    mine = merged[0].astype(F32)
    for s in range(1, nz):
        mine = mine + hop(merged[s], dz=s).astype(F32)
    mine, frame_grad = lax.optimization_barrier((mine.astype(BF16), frame_grad))
    block = lambda kind: jax.ShapeDtypeStruct((2 * quests * nq, part), kind)
    blocks = call(
        functools.partial(project_kernel, cols=cols),
        (block(F32),) + (block(BF16),) * (shards - 1),
        "svv",
        "v" * shards,
        mib=2,
    )(shard.astype(jnp.int32).reshape(1), mine, w_q_out)
    both = blocks[0]
    for s in range(1, shards):
        both = both + mp_hop(blocks[s], s).astype(F32)
    both = both.astype(BF16).reshape(2, quests, nq, part)
    return both[0], both[1], frame_grad


def solution(mesh):
    placed = (
        P("frames", None, None),
        P("frames", None),
        P("frames", None, None),
        P(None, "mp"),
        P(None, "mp"),
        P(None, "mp"),
        P("mp", None),
        P("frames", None, None),
    )
    return jax.shard_map(
        body,
        mesh=mesh,
        in_specs=placed,
        out_specs=(P("frames", None, "mp"), P("frames", None, "mp"), P("frames", None, "mp")),
        check_vma=False,
    )
```

```python
import functools

import jax
import jax.numpy as jnp
from jax import lax
from jax.experimental import pallas as pl
from jax.experimental.pallas import tpu as pltpu
from jax.sharding import PartitionSpec as P

HEAD_DIM = 64
NT = (((1,), (1,)), ((), ()))
TN = (((0,), (0,)), ((), ()))
NN = (((1,), (0,)), ((), ()))
F32 = jnp.float32
BF16 = jnp.bfloat16


def dot(a, b, dims):
    return lax.dot_general(a, b, dims, preferred_element_type=F32)


def head_masks(heads, wide):
    lane = lax.broadcasted_iota(jnp.int32, (1, wide), 1) // HEAD_DIM
    low = [(lane == h).astype(BF16) for h in range(heads)]
    high = [(lane == h + 1).astype(BF16) for h in range(heads)]
    return low, high


def spread(block, masks):
    return jnp.concatenate([block * m for m in masks], axis=0)


def gathered(block, masks, nq):
    total = block[:nq] * masks[0].astype(F32)
    for h in range(1, len(masks)):
        total = total + block[h * nq:(h + 1) * nq] * masks[h].astype(F32)
    return total


AXES = (4, 8, 2)
FIRST = 3


def frames_perm(dx=0, dz=0, dc=0):
    nx, nz, nc = AXES
    pairs = []
    for x in range(nx):
        for z in range(nz):
            for c in range(nc):
                to = (((x + dx) % nx) * nz + (z + dz) % nz) * nc + (c + dc) % nc
                pairs.append(((x * nz + z) * nc + c, to))
    return pairs


def planes():
    nx, nz, nc = AXES
    number = lambda x, z, c: (x * nz + z) * nc + c
    flat = [[number(x, z, c) for x in range(nx) for c in range(nc)] for z in range(nz)]
    line = [[number(x, z, c) for z in range(nz)] for x in range(nx) for c in range(nc)]
    return flat, line


def hop(value, **shift):
    return lax.ppermute(value, "frames", frames_perm(**shift))


def plan_kernel(codes_ref, me_ref, order_ref, size_ref, at_ref, *, cap, quests, nq, tok, frames_here):
    nx, nz, nc = AXES
    owners = nx * nz * nc
    bits = frames_here.bit_length() - 1
    me = me_ref[0]
    x, z, c = lax.div(me, nz * nc), lax.rem(lax.div(me, nc), nz), lax.rem(me, nc)

    def step(block, found):
        at, core, across = lax.div(block, nc * nx), lax.rem(lax.div(block, nx), nc), lax.rem(block, nx)
        away = jnp.where(lax.rem(at, 2) == 1, lax.div(at + 1, 2), nz - lax.div(at, 2))
        there = lax.rem(x - across + nx, nx) * nz + lax.rem(z - away + nz, nz)
        src = there * nc + lax.rem(c + core, nc)
        asks = (lax.rem(there, nz) * nx + lax.div(there, nz)) * nc + lax.rem(c + core, nc)
        valid = codes_ref[asks * cap] > 0
        order_ref[jnp.where(valid, found, owners - 1 - (block - found))] = src
        for r in range(cap):
            code = jnp.maximum(codes_ref[asks * cap + r] - 1, 0)
            row = (block * quests + (code >> bits)) * nq
            at_ref[src * cap + r] = jnp.where(valid, row, 0)
            at_ref[(owners + src) * cap + r] = (code & (frames_here - 1)) * tok
        return found + jnp.where(valid, 1, 0)

    near = lax.fori_loop(0, FIRST * nx * nc, step, 0)
    size_ref[1] = near
    size_ref[0] = lax.fori_loop(FIRST * nx * nc, owners, step, near)


def load_rows(pieces, x_ref, sems):
    copies, row = [], 0
    full = pieces[0].shape[0]
    for i, piece in enumerate(pieces):
        size = piece.shape[0]
        if size == full:
            row = i * full
        else:
            half, core = divmod(i - (len(pieces) - 4), 2)
            row = (len(pieces) - 4 + core) * full + half * size
        copies.append(pltpu.make_async_copy(piece, x_ref.at[pl.ds(row, size)], sems.at[i]))
        copies[-1].start()
    return copies


def in_groups(order_ref, size_ref, copies, group, step):
    early = size_ref[1] // group
    for c in copies[:2 * FIRST]:
        c.wait()
    lax.fori_loop(0, early, step, 0)
    for c in copies[2 * FIRST:]:
        c.wait()
    last = (size_ref[0] + group - 1) // group
    lax.fori_loop(early, last, step, 0)
    return last


def group_of(i, group, cap, order_ref):
    srcs = [order_ref[i * group + g] for g in range(group)]
    return srcs, [src * cap + r for src in srcs for r in range(cap)]


def rows_of(at_ref, slots, x_ref, kv_ref, nq, tok, low, high):
    at = [pl.multiple_of(at_ref[slot], nq) for slot in slots]
    keys = [pl.multiple_of(at_ref[at_ref.shape[0] // 2 + slot], tok) for slot in slots]
    qm = [spread(x_ref[pl.ds(a, nq), 0:256], low) for a in at]
    dm = [spread(x_ref[pl.ds(a, nq), 128:384], high) for a in at]
    k = [kv_ref[pl.ds(a, tok), 0:256] for a in keys]
    v = [kv_ref[pl.ds(a, tok), 128:384] for a in keys]
    s = [dot(a, b, NT) for a, b in zip(k, qm)]
    dp = [dot(a, b, NT) for a, b in zip(v, dm)]
    return s, dp, qm, dm, k, v, keys


def stats_kernel(order_ref, size_ref, at_ref, kv_ref, *refs, cap, nq, tok, heads, group):
    *pieces, out_ref, x_ref, sems = refs
    low, high = head_masks(heads, 256)
    copies = load_rows(pieces, x_ref, sems)
    wide = heads * nq

    def step(i, carry):
        srcs, slots = group_of(i, group, cap, order_ref)
        s, dp, *_ = rows_of(at_ref, slots, x_ref, kv_ref, nq, tok, low, high)
        m = [jnp.max(a, axis=0, keepdims=True) for a in s]
        e = [jnp.exp(a - b) for a, b in zip(s, m)]
        for n, (a, b, c) in enumerate(zip(m, e, dp)):
            src, r = srcs[n // cap], 3 * (n % cap)
            out_ref[src, r:r + 1, 0:wide] = a
            out_ref[src, r + 1:r + 2, 0:wide] = jnp.sum(b, axis=0, keepdims=True)
            out_ref[src, r + 2:r + 3, 0:wide] = jnp.sum(b * c, axis=0, keepdims=True)
        return carry

    in_groups(order_ref, size_ref, copies, group, step)


def combine_kernel(quest_ref, st_ref, out_ref, *, cap, quests):
    ids = [quest_ref[r] for r in range(cap)]
    top = [st_ref[:, 3 * r, :] for r in range(cap)]
    size = [st_ref[:, 3 * r + 1, :] for r in range(cap)]
    mean = [st_ref[:, 3 * r + 2, :] for r in range(cap)]
    none = jnp.zeros_like(top[0])
    outs = [[none + 3e38, none, none] for _ in range(cap)]
    for j in range(quests):
        on = [ids[r] == j for r in range(cap)]
        big = functools.reduce(
            jnp.maximum,
            [jnp.max(jnp.where(on[r], top[r], -jnp.inf), axis=0, keepdims=True) for r in range(cap)],
        )
        norm, delta = 0.0, 0.0
        for r in range(cap):
            e = jnp.exp(top[r] - big)
            norm = norm + jnp.sum(jnp.where(on[r], e * size[r], 0.0), axis=0, keepdims=True)
            delta = delta + jnp.sum(jnp.where(on[r], e * mean[r], 0.0), axis=0, keepdims=True)
        inv = 1.0 / norm
        for r in range(cap):
            for i, val in enumerate((big, inv, delta * inv)):
                outs[r][i] = jnp.where(on[r], val, outs[r][i])
    for r in range(cap):
        for i in range(3):
            out_ref[:, 3 * r + i, :] = outs[r][i]


def main_kernel(
    order_ref, size_ref, at_ref, kv_ref, st_ref, x_ref, ret_ref, sum_ref, acc_ref,
    *, cap, nq, tok, heads, group, scale
):
    low, high = head_masks(heads, 256)
    acc_ref[...] = jnp.zeros_like(acc_ref)
    wide = heads * nq
    size = cap * nq

    nx, nz, nc = AXES

    def place(src):
        column = lax.div(src, nz * nc) * nc + lax.rem(src, nc)
        return pl.multiple_of((column * nz + lax.rem(lax.div(src, nc), nz)) * size, size)

    def step(i, carry):
        srcs, slots = group_of(i, group, cap, order_ref)
        s, dp, qm, dm, k, v, keys = rows_of(at_ref, slots, x_ref, kv_ref, nq, tok, low, high)
        st = [
            [st_ref[src, 3 * r + n:3 * r + n + 1, 0:wide] for n in range(3)] for src in srcs for r in range(cap)
        ]
        p = [jnp.exp(a - b[0]) * b[1] for a, b in zip(s, st)]
        w = [a.astype(BF16) for a in p]
        ds = [(a * (b - c[2])).astype(BF16) for a, b, c in zip(p, dp, st)]
        o = [gathered(dot(a, b, TN), high, nq) for a, b in zip(w, v)]
        dq = [gathered(dot(a, b, TN), low, nq) * scale for a, b in zip(ds, k)]
        dk = [dot(a, b, NN) for a, b in zip(ds, qm)]
        dv = [dot(a, b, NN) for a, b in zip(w, dm)]
        for n in range(len(slots)):
            row = pl.ds(pl.multiple_of(place(srcs[n // cap]) + n % cap * nq, nq), nq)
            ret_ref[row, 0:128] = dq[n][:, 0:128].astype(BF16)
            ret_ref[row, 128:256] = (dq[n][:, 128:256] + o[n][:, 0:128]).astype(BF16)
            ret_ref[row, 256:384] = o[n][:, 128:256].astype(BF16)
            at = pl.ds(keys[n], tok)
            acc_ref[at, 0:128] += dk[n][:, 0:128]
            acc_ref[at, 128:256] += dk[n][:, 128:256] + dv[n][:, 0:128]
            acc_ref[at, 256:384] += dv[n][:, 128:256]
        return carry

    last = (size_ref[0] + group - 1) // group
    lax.fori_loop(0, last, step, 0)

    def rest(i, carry):
        src = order_ref[i]
        ret_ref[pl.ds(place(src), size), :] = jnp.zeros((size, ret_ref.shape[1]), BF16)
        return carry

    lax.fori_loop(last * group, order_ref.shape[0], rest, 0)
    sum_ref[...] = acc_ref[...].astype(BF16)


def merge_kernel(me_ref, pick_ref, ret_ref, *out_refs):
    nz = len(out_refs)
    for s, out_ref in enumerate(out_refs):
        to = lax.rem(me_ref[0] + s, nz)
        rows = jnp.concatenate([ret_ref[u, to] for u in range(ret_ref.shape[0])], axis=0)
        out_ref[...] = dot(pick_ref[to], rows, NN).astype(BF16)


def project_kernel(x_ref, w_ref, out_ref, *, cols):
    lane = lax.broadcasted_iota(jnp.int32, (1, 256), 1)
    grad = x_ref[:, 0:256] * (lane < cols).astype(BF16)
    mixed = x_ref[:, 128:384] * (lane >= cols - 128).astype(BF16)
    rows = x_ref.shape[0]
    many = out_ref.shape[0]
    part = w_ref.shape[0] // many
    for to in range(many):
        at = pl.ds(to * part, part)
        out_ref[to, 0:rows, :] = dot(mixed, w_ref[at, 128:384], NT).astype(out_ref.dtype)
        out_ref[to, rows:2 * rows, :] = dot(grad, w_ref[at, 0:256], NT).astype(out_ref.dtype)


def call(kernel, out_shape, ins, outs, scratch=(), mib=1):
    spaces = {"s": pltpu.SMEM, "v": pltpu.VMEM, "a": pltpu.HBM}
    out_specs = [pl.BlockSpec(memory_space=spaces[i]) for i in outs]
    return pl.pallas_call(
        kernel,
        out_shape=out_shape,
        in_specs=[pl.BlockSpec(memory_space=spaces[i]) for i in ins],
        out_specs=out_specs if len(outs) > 1 else out_specs[0],
        scratch_shapes=list(scratch),
        compiler_params=pltpu.CompilerParams(vmem_limit_bytes=mib * 1024 * 1024),
    )


def mp_hop(value, s):
    many = lax.axis_size("mp")
    return lax.ppermute(value, "mp", [(i, (i + s) % many) for i in range(many)])


def body(frames, keyframes, query_states, w_query, w_key, w_value, w_out, out_grad):
    owners = lax.axis_size("frames")
    shards = lax.axis_size("mp")
    me, shard = lax.axis_index("frames"), lax.axis_index("mp")
    fr_count, tok, width = frames.shape
    quests, keys = keyframes.shape
    nq = query_states.shape[1]
    hid = query_states.shape[2]
    cols = w_key.shape[1]
    heads = cols // HEAD_DIM
    scale = HEAD_DIM ** (-0.5)
    count = quests * keys
    cap = max(2, count // owners)
    group = 4

    queries = jnp.dot(query_states.reshape(quests * nq, hid), w_query, preferred_element_type=F32)
    d_mixed = lax.dot_general(out_grad.reshape(quests * nq, hid), w_out, NT, preferred_element_type=F32)
    local = jnp.concatenate([queries.astype(BF16) * scale, d_mixed.astype(BF16)], axis=1)
    picks = keyframes.reshape(-1)
    owner = picks >> (fr_count.bit_length() - 1)
    position = jnp.arange(count)
    same = owner[:, None] == owner[None, :]
    rank = jnp.sum(jnp.logical_and(same, position[None, :] < position[:, None]), axis=1)
    code = (picks & (fr_count - 1)) + fr_count * (position // keys) + 1
    slot = owner * cap + rank
    requests = jnp.sum(
        jnp.where(slot[None, :] == jnp.arange(owners * cap)[:, None], code[None, :], 0), axis=1
    ).astype(jnp.int32)
    asked = jnp.where(requests > 0, (requests - 1) >> (fr_count.bit_length() - 1), -1)
    quest_of = jnp.broadcast_to(asked.reshape(owners, cap).T[:, :, None], (cap, owners, 128))

    nx, nz, nc = AXES
    owners = nx * nz * nc
    bits = frames_here.bit_length() - 1
    me = me_ref[0]
    x, z, c = lax.div(me, nz * nc), lax.rem(lax.div(me, nc), nz), lax.rem(me, nc)

    def step(block, found):
        at, core, across = lax.div(block, nc * nx), lax.rem(lax.div(block, nx), nc), lax.rem(block, nx)
        away = jnp.where(lax.rem(at, 2) == 1, lax.div(at + 1, 2), nz - lax.div(at, 2))
        there = lax.rem(x - across + nx, nx) * nz + lax.rem(z - away + nz, nz)
        src = there * nc + lax.rem(c + core, nc)
        asks = (lax.rem(there, nz) * nx + lax.div(there, nz)) * nc + lax.rem(c + core, nc)
        valid = codes_ref[asks * cap] > 0
        order_ref[jnp.where(valid, found, owners - 1 - (block - found))] = src
        for r in range(cap):
            code = jnp.maximum(codes_ref[asks * cap + r] - 1, 0)
            row = (block * quests + (code >> bits)) * nq
            at_ref[src * cap + r] = jnp.where(valid, row, 0)
            at_ref[(owners + src) * cap + r] = (code & (frames_here - 1)) * tok
        return found + jnp.where(valid, 1, 0)

    near = lax.fori_loop(0, FIRST * nx * nc, step, 0)
    size_ref[1] = near
    size_ref[0] = lax.fori_loop(FIRST * nx * nc, owners, step, near)


def load_rows(pieces, x_ref, sems):
    copies, row = [], 0
    full = pieces[0].shape[0]
    for i, piece in enumerate(pieces):
        size = piece.shape[0]
        if size == full:
            row = i * full
        else:
            half, core = divmod(i - (len(pieces) - 4), 2)
            row = (len(pieces) - 4 + core) * full + half * size
        copies.append(pltpu.make_async_copy(piece, x_ref.at[pl.ds(row, size)], sems.at[i]))
        copies[-1].start()
    return copies


def in_groups(order_ref, size_ref, copies, group, step):
    early = size_ref[1] // group
    for c in copies[:2 * FIRST]:
        c.wait()
    lax.fori_loop(0, early, step, 0)
    for c in copies[2 * FIRST:]:
        c.wait()
    last = (size_ref[0] + group - 1) // group
    lax.fori_loop(early, last, step, 0)
    return last


def group_of(i, group, cap, order_ref):
    srcs = [order_ref[i * group + g] for g in range(group)]
    return srcs, [src * cap + r for src in srcs for r in range(cap)]


def rows_of(at_ref, slots, x_ref, kv_ref, nq, tok, low, high):
    at = [pl.multiple_of(at_ref[slot], nq) for slot in slots]
    keys = [pl.multiple_of(at_ref[at_ref.shape[0] // 2 + slot], tok) for slot in slots]
    qm = [spread(x_ref[pl.ds(a, nq), 0:256], low) for a in at]
    dm = [spread(x_ref[pl.ds(a, nq), 128:384], high) for a in at]
    k = [kv_ref[pl.ds(a, tok), 0:256] for a in keys]
    v = [kv_ref[pl.ds(a, tok), 128:384] for a in keys]
    s = [dot(a, b, NT) for a, b in zip(k, qm)]
    dp = [dot(a, b, NT) for a, b in zip(v, dm)]
    return s, dp, qm, dm, k, v, keys


def stats_kernel(order_ref, size_ref, at_ref, kv_ref, *refs, cap, nq, tok, heads, group):
    *pieces, out_ref, x_ref, sems = refs
    low, high = head_masks(heads, 256)
    copies = load_rows(pieces, x_ref, sems)
    wide = heads * nq

    def step(i, carry):
        srcs, slots = group_of(i, group, cap, order_ref)
        s, dp, *_ = rows_of(at_ref, slots, x_ref, kv_ref, nq, tok, low, high)
        m = [jnp.max(a, axis=0, keepdims=True) for a in s]
        e = [jnp.exp(a - b) for a, b in zip(s, m)]
        for n, (a, b, c) in enumerate(zip(m, e, dp)):
            src, r = srcs[n // cap], 3 * (n % cap)
            out_ref[src, r:r + 1, 0:wide] = a
            out_ref[src, r + 1:r + 2, 0:wide] = jnp.sum(b, axis=0, keepdims=True)
            out_ref[src, r + 2:r + 3, 0:wide] = jnp.sum(b * c, axis=0, keepdims=True)
        return carry

    in_groups(order_ref, size_ref, copies, group, step)


def combine_kernel(quest_ref, st_ref, out_ref, *, cap, quests):
    ids = [quest_ref[r] for r in range(cap)]
    top = [st_ref[:, 3 * r, :] for r in range(cap)]
    size = [st_ref[:, 3 * r + 1, :] for r in range(cap)]
    mean = [st_ref[:, 3 * r + 2, :] for r in range(cap)]
    none = jnp.zeros_like(top[0])
    outs = [[none + 3e38, none, none] for _ in range(cap)]
    for j in range(quests):
        on = [ids[r] == j for r in range(cap)]
        big = functools.reduce(
            jnp.maximum,
            [jnp.max(jnp.where(on[r], top[r], -jnp.inf), axis=0, keepdims=True) for r in range(cap)],
        )
        norm, delta = 0.0, 0.0
        for r in range(cap):
            e = jnp.exp(top[r] - big)
            norm = norm + jnp.sum(jnp.where(on[r], e * size[r], 0.0), axis=0, keepdims=True)
            delta = delta + jnp.sum(jnp.where(on[r], e * mean[r], 0.0), axis=0, keepdims=True)
        inv = 1.0 / norm
        for r in range(cap):
            for i, val in enumerate((big, inv, delta * inv)):
                outs[r][i] = jnp.where(on[r], val, outs[r][i])
    for r in range(cap):
        for i in range(3):
            out_ref[:, 3 * r + i, :] = outs[r][i]


def main_kernel(
    order_ref, size_ref, at_ref, kv_ref, st_ref, x_ref, ret_ref, sum_ref, acc_ref,
    *, cap, nq, tok, heads, group, scale
):
    low, high = head_masks(heads, 256)
    acc_ref[...] = jnp.zeros_like(acc_ref)
    wide = heads * nq
    size = cap * nq

    nx, nz, nc = AXES

    def place(src):
        column = lax.div(src, nz * nc) * nc + lax.rem(src, nc)
        return pl.multiple_of((column * nz + lax.rem(lax.div(src, nc), nz)) * size, size)

    def step(i, carry):
        srcs, slots = group_of(i, group, cap, order_ref)
        s, dp, qm, dm, k, v, keys = rows_of(at_ref, slots, x_ref, kv_ref, nq, tok, low, high)
        st = [
            [st_ref[src, 3 * r + n:3 * r + n + 1, 0:wide] for n in range(3)] for src in srcs for r in range(cap)
        ]
        p = [jnp.exp(a - b[0]) * b[1] for a, b in zip(s, st)]
        w = [a.astype(BF16) for a in p]
        ds = [(a * (b - c[2])).astype(BF16) for a, b, c in zip(p, dp, st)]
        o = [gathered(dot(a, b, TN), high, nq) for a, b in zip(w, v)]
        dq = [gathered(dot(a, b, TN), low, nq) * scale for a, b in zip(ds, k)]
        dk = [dot(a, b, NN) for a, b in zip(ds, qm)]
        dv = [dot(a, b, NN) for a, b in zip(w, dm)]
        for n in range(len(slots)):
            row = pl.ds(pl.multiple_of(place(srcs[n // cap]) + n % cap * nq, nq), nq)
            ret_ref[row, 0:128] = dq[n][:, 0:128].astype(BF16)
            ret_ref[row, 128:256] = (dq[n][:, 128:256] + o[n][:, 0:128]).astype(BF16)
            ret_ref[row, 256:384] = o[n][:, 128:256].astype(BF16)
            at = pl.ds(keys[n], tok)
            acc_ref[at, 0:128] += dk[n][:, 0:128]
            acc_ref[at, 128:256] += dk[n][:, 128:256] + dv[n][:, 0:128]
            acc_ref[at, 256:384] += dv[n][:, 128:256]
        return carry

    last = (size_ref[0] + group - 1) // group
    lax.fori_loop(0, last, step, 0)

    def rest(i, carry):
        src = order_ref[i]
        ret_ref[pl.ds(place(src), size), :] = jnp.zeros((size, ret_ref.shape[1]), BF16)
        return carry

    lax.fori_loop(last * group, order_ref.shape[0], rest, 0)
    sum_ref[...] = acc_ref[...].astype(BF16)


def merge_kernel(me_ref, pick_ref, ret_ref, *out_refs):
    nz = len(out_refs)
    for s, out_ref in enumerate(out_refs):
        to = lax.rem(me_ref[0] + s, nz)
        rows = jnp.concatenate([ret_ref[u, to] for u in range(ret_ref.shape[0])], axis=0)
        out_ref[...] = dot(pick_ref[to], rows, NN).astype(BF16)


def finish_kernel(*refs, cols):
    *ins, att_ref, grad_ref = refs
    many = len(ins) // 2
    lane = lax.broadcasted_iota(jnp.int32, (1, 256), 1)
    low = (lane < cols).astype(BF16)
    high = (lane >= cols - 128).astype(BF16)
    att, grad = 0.0, 0.0
    for x_ref, w_ref in zip(ins[:many], ins[many:]):
        grad = grad + dot(x_ref[:, 0:256] * low, w_ref[:, 0:256], NT)
        att = att + dot(x_ref[:, 128:384] * high, w_ref[:, 128:384], NT)
    att_ref[...] = att.astype(BF16)
    grad_ref[...] = grad.astype(BF16)


def call(kernel, out_shape, ins, outs, scratch=(), mib=1):
    spaces = {"s": pltpu.SMEM, "v": pltpu.VMEM, "a": pltpu.HBM}
    out_specs = [pl.BlockSpec(memory_space=spaces[i]) for i in outs]
    return pl.pallas_call(
        kernel,
        out_shape=out_shape,
        in_specs=[pl.BlockSpec(memory_space=spaces[i]) for i in ins],
        out_specs=out_specs if len(outs) > 1 else out_specs[0],
        scratch_shapes=list(scratch),
        compiler_params=pltpu.CompilerParams(vmem_limit_bytes=mib * 1024 * 1024),
    )


def mp_hop(value, s):
    many = lax.axis_size("mp")
    return lax.ppermute(value, "mp", [(i, (i + s) % many) for i in range(many)])


def body(frames, keyframes, query_states, w_query, w_key, w_value, w_out, out_grad):
    owners = lax.axis_size("frames")
    shards = lax.axis_size("mp")
    me, shard = lax.axis_index("frames"), lax.axis_index("mp")
    fr_count, tok, width = frames.shape
    quests, keys = keyframes.shape
    nq = query_states.shape[1]
    hid = query_states.shape[2]
    cols = w_key.shape[1]
    heads = cols // HEAD_DIM
    scale = HEAD_DIM ** (-0.5)
    count = quests * keys
    cap = max(2, count // owners)
    group = 4

    queries = jnp.dot(query_states.reshape(quests * nq, hid), w_query, preferred_element_type=F32)
    d_mixed = lax.dot_general(out_grad.reshape(quests * nq, hid), w_out, NT, preferred_element_type=F32)
    local = jnp.concatenate([queries.astype(BF16) * scale, d_mixed.astype(BF16)], axis=1)
    picks = keyframes.reshape(-1)
    owner = picks >> (fr_count.bit_length() - 1)
    position = jnp.arange(count)
    same = owner[:, None] == owner[None, :]
    rank = jnp.sum(jnp.logical_and(same, position[None, :] < position[:, None]), axis=1)
    code = (picks & (fr_count - 1)) + fr_count * (position // keys) + 1
    slot = owner * cap + rank
    requests = jnp.sum(
        jnp.where(slot[None, :] == jnp.arange(owners * cap)[:, None], code[None, :], 0), axis=1
    ).astype(jnp.int32)
    asked = jnp.where(requests > 0, (requests - 1) >> (fr_count.bit_length() - 1), -1)
    quest_of = jnp.broadcast_to(asked.reshape(owners, cap).T[:, :, None], (cap, owners, 128))
    put = jnp.arange(quests * nq)[:, None]
    take = jnp.arange(owners * cap * nq)[None, :]
    pick_sum = jnp.logical_and(put // nq == jnp.repeat(asked, nq)[None, :], put % nq == take % nq).astype(BF16)

    w_both = jnp.concatenate([w_key, w_value], axis=1)
    bank = jnp.dot(frames.reshape(fr_count * tok, width), w_both, preferred_element_type=F32).astype(BF16)
    flat, line = planes()
    nx, nz, nc = AXES
    mine = jnp.concatenate([local] + [hop(local, dx=s) for s in range(1, nx)], axis=0)
    passed = requests.reshape(nx, nz, nc, cap).swapaxes(0, 1).reshape(nz, nx * nc * cap)
    passed = lax.all_to_all(passed, "frames", 0, 0, axis_index_groups=line, tiled=True)
    mine, passed, bank = lax.optimization_barrier((mine, passed, bank))
    incoming = passed.reshape(nz, nx * nc, cap).swapaxes(0, 1).reshape(nx * nc, nz * cap)
    incoming = lax.all_to_all(incoming, "frames", 0, 0, axis_index_groups=flat, tiled=True)
    incoming = incoming.reshape(nx * nc, nz, cap).swapaxes(0, 1).reshape(-1)
    ways = [(mine, mine)]
    ways.append((hop(ways[-1][0], dz=1), hop(ways[-1][1], dz=-1)))
    ways[-1], incoming = lax.optimization_barrier((ways[-1], incoming))
    ints = lambda *shape: jax.ShapeDtypeStruct(shape, jnp.int32)
    order, sizes, at = call(
        functools.partial(plan_kernel, cap=cap, quests=quests, nq=nq, tok=tok, frames_here=fr_count),
        (ints(owners), ints(2), ints(2 * owners * cap)),
        "ss",
        "sss",
    )(incoming, me.astype(jnp.int32).reshape(1))
    ways.append((hop(ways[-1][0], dz=1), hop(ways[-1][1], dz=-1)))
    ways[-1], order, sizes, at, quest_of = lax.optimization_barrier((ways[-1], order, sizes, at, quest_of))
    ways.append((hop(ways[-1][0], dz=1), hop(ways[-1][1], dz=-1)))
    half = mine.shape[0] // 2
    pieces = [mine] + [way for pair in ways[1:] for way in pair]
    pieces += [hop(ways[-1][0][:half], dz=1), hop(ways[-1][1][half:], dz=-1)]
    pieces = [p for piece in pieces for p in (piece, hop(piece, dc=1))]

    dims = dict(cap=cap, nq=nq, tok=tok, heads=heads, group=group)
    held = (owners * cap * nq, 2 * cols)
    stat_shape = jax.ShapeDtypeStruct((owners, 8, 128), F32)
    rows = jax.ShapeDtypeStruct((owners * quests * nq, 2 * cols), BF16)
    stats, rows = call(
        functools.partial(stats_kernel, **dims),
        (stat_shape, rows),
        "sssv" + "a" * len(pieces),
        "vv",
        [pltpu.SemaphoreType.DMA((len(pieces),))],
        4,
    )(order, sizes, at, bank, *pieces)
    stats = lax.all_to_all(stats, "frames", split_axis=0, concat_axis=0, tiled=True)
    stats = call(functools.partial(combine_kernel, cap=cap, quests=quests), stat_shape, "vv", "v")(quest_of, stats)
    stats = lax.all_to_all(stats, "frames", split_axis=0, concat_axis=0, tiled=True)
    partial, sums = call(
        functools.partial(main_kernel, scale=scale, **dims),
        (jax.ShapeDtypeStruct(held, BF16), jax.ShapeDtypeStruct((fr_count * tok, 2 * cols), BF16)),
        "sssvvv",
        "vv",
        [pltpu.VMEM((fr_count * tok, 2 * cols), F32)],
        8,
    )(order, sizes, at, bank, stats, rows)
    partial = lax.all_to_all(
        partial.reshape(nx * nc, nz * cap * nq, 2 * cols), "frames", 0, 0, axis_index_groups=flat, tiled=True
    ).reshape(nx * nc, nz, cap * nq, 2 * cols)
    asked = jnp.where(passed > 0, (passed - 1) >> (fr_count.bit_length() - 1), -1)
    put = jnp.arange(quests * nq)[None, :, None]
    take = jnp.arange(nx * nc * cap * nq)[None, None, :]
    asked = jnp.repeat(asked.reshape(nz, 1, nx * nc * cap), nq, axis=2)
    pick_sum = jnp.logical_and(put // nq == asked, put % nq == take % nq).astype(BF16)

    w_q_out = jnp.concatenate([w_query, w_out.T], axis=1)
    own = [(shard + s) % shards for s in range(shards)]
    part = hid // shards
    slab = width // shards
    terms = [
        lax.dot_general(
            sums, lax.dynamic_slice_in_dim(w_both, own[s] * slab, slab, 0), NT, preferred_element_type=F32
        )
        for s in range(shards)
    ]
    frame_grad = terms[0]
    for s in range(1, shards):
        frame_grad = frame_grad + mp_hop(terms[s].astype(BF16), s).astype(F32)

    frame_grad = frame_grad.astype(BF16).reshape(fr_count, tok, slab)
    partial, w_q_out, pick_sum = lax.optimization_barrier((partial, w_q_out, pick_sum))
    mine_shape = jax.ShapeDtypeStruct((quests * nq, 2 * cols), BF16)
    merged = call(merge_kernel, (mine_shape,) * nz, "svv", "v" * nz, mib=4)(
        lax.rem(lax.div(me, nc), nz).astype(jnp.int32).reshape(1), pick_sum, partial
    )
    mine = merged[0].astype(F32)
    for s in range(1, nz):
        mine = mine + hop(merged[s], dz=s).astype(F32)
    mine, frame_grad = lax.optimization_barrier((mine.astype(BF16), frame_grad))
    blocks = call(
        functools.partial(project_kernel, cols=cols),
        jax.ShapeDtypeStruct((shards, 2 * quests * nq, part), BF16),
        "vv",
        "v",
        mib=2,
    )(mine, w_q_out)
    blocks = lax.all_to_all(blocks, "mp", 0, 0, tiled=True)
    both = jnp.sum(blocks.astype(F32), axis=0).astype(BF16).reshape(2, quests, nq, part)
    return both[0], both[1], frame_grad


def solution(mesh):
    placed = (
        P("frames", None, None),
        P("frames", None),
        P("frames", None, None),
        P(None, "mp"),
        P(None, "mp"),
        P(None, "mp"),
        P("mp", None),
        P("frames", None, None),
    )
    return jax.shard_map(
        body,
        mesh=mesh,
        in_specs=placed,
        out_specs=(P("frames", None, "mp"), P("frames", None, "mp"), P("frames", None, "mp")),
        check_vma=False,
    )
```

```python
import functools

import jax
import jax.numpy as jnp
from jax import lax
from jax.experimental import pallas as pl
from jax.experimental.pallas import tpu as pltpu
from jax.sharding import PartitionSpec as P

HEAD_DIM = 64
NT = (((1,), (1,)), ((), ()))
TN = (((0,), (0,)), ((), ()))
NN = (((1,), (0,)), ((), ()))
F32 = jnp.float32
BF16 = jnp.bfloat16


def dot(a, b, dims):
    return lax.dot_general(a, b, dims, preferred_element_type=F32)


def head_masks(heads, wide):
    lane = lax.broadcasted_iota(jnp.int32, (1, wide), 1) // HEAD_DIM
    low = [(lane == h).astype(BF16) for h in range(heads)]
    high = [(lane == h + 1).astype(BF16) for h in range(heads)]
    return low, high


def spread(block, masks):
    return jnp.concatenate([block * m for m in masks], axis=0)


def gathered(block, masks, nq):
    total = block[:nq] * masks[0].astype(F32)
    for h in range(1, len(masks)):
        total = total + block[h * nq:(h + 1) * nq] * masks[h].astype(F32)
    return total


AXES = (4, 8, 2)
FIRST = 3


def frames_perm(dx=0, dz=0, dc=0):
    nx, nz, nc = AXES
    pairs = []
    for x in range(nx):
        for z in range(nz):
            for c in range(nc):
                to = (((x + dx) % nx) * nz + (z + dz) % nz) * nc + (c + dc) % nc
                pairs.append(((x * nz + z) * nc + c, to))
    return pairs


def planes():
    nx, nz, nc = AXES
    number = lambda x, z, c: (x * nz + z) * nc + c
    flat = [[number(x, z, c) for x in range(nx) for c in range(nc)] for z in range(nz)]
    line = [[number(x, z, c) for z in range(nz)] for x in range(nx) for c in range(nc)]
    return flat, line


def hop(value, **shift):
    return lax.ppermute(value, "frames", frames_perm(**shift))


def plan_kernel(codes_ref, me_ref, order_ref, size_ref, at_ref, *, cap, quests, nq, tok, frames_here):
    nx, nz, nc = AXES
    owners = nx * nz * nc
    bits = frames_here.bit_length() - 1
    me = me_ref[0]
    x, z, c = lax.div(me, nz * nc), lax.rem(lax.div(me, nc), nz), lax.rem(me, nc)

    def step(block, found):
        at, core, across = lax.div(block, nc * nx), lax.rem(lax.div(block, nx), nc), lax.rem(block, nx)
        away = jnp.where(lax.rem(at, 2) == 1, lax.div(at + 1, 2), nz - lax.div(at, 2))
        there = lax.rem(x - across + nx, nx) * nz + lax.rem(z - away + nz, nz)
        src = there * nc + lax.rem(c + core, nc)
        asks = (lax.rem(there, nz) * nx + lax.div(there, nz)) * nc + lax.rem(c + core, nc)
        valid = codes_ref[asks * cap] > 0
        order_ref[jnp.where(valid, found, owners - 1 - (block - found))] = src
        for r in range(cap):
            code = jnp.maximum(codes_ref[asks * cap + r] - 1, 0)
            row = (block * quests + (code >> bits)) * nq
            at_ref[src * cap + r] = jnp.where(valid, row, 0)
            at_ref[(owners + src) * cap + r] = (code & (frames_here - 1)) * tok
        return found + jnp.where(valid, 1, 0)

    near = lax.fori_loop(0, FIRST * nx * nc, step, 0)
    size_ref[1] = near
    size_ref[0] = lax.fori_loop(FIRST * nx * nc, owners, step, near)


def load_rows(pieces, x_ref, sems):
    copies, row = [], 0
    full = pieces[0].shape[0]
    for i, piece in enumerate(pieces):
        size = piece.shape[0]
        if size == full:
            row = i * full
        else:
            half, core = divmod(i - (len(pieces) - 4), 2)
            row = (len(pieces) - 4 + core) * full + half * size
        copies.append(pltpu.make_async_copy(piece, x_ref.at[pl.ds(row, size)], sems.at[i]))
        copies[-1].start()
    return copies


def in_groups(order_ref, size_ref, copies, group, step):
    early = size_ref[1] // group
    for c in copies[:2 * FIRST]:
        c.wait()
    lax.fori_loop(0, early, step, 0)
    for c in copies[2 * FIRST:]:
        c.wait()
    last = (size_ref[0] + group - 1) // group
    lax.fori_loop(early, last, step, 0)
    return last


def group_of(i, group, cap, order_ref):
    srcs = [order_ref[i * group + g] for g in range(group)]
    return srcs, [src * cap + r for src in srcs for r in range(cap)]


def rows_of(at_ref, slots, x_ref, kv_ref, nq, tok, low, high):
    at = [pl.multiple_of(at_ref[slot], nq) for slot in slots]
    keys = [pl.multiple_of(at_ref[at_ref.shape[0] // 2 + slot], tok) for slot in slots]
    qm = [spread(x_ref[pl.ds(a, nq), 0:256], low) for a in at]
    dm = [spread(x_ref[pl.ds(a, nq), 128:384], high) for a in at]
    k = [kv_ref[pl.ds(a, tok), 0:256] for a in keys]
    v = [kv_ref[pl.ds(a, tok), 128:384] for a in keys]
    s = [dot(a, b, NT) for a, b in zip(k, qm)]
    dp = [dot(a, b, NT) for a, b in zip(v, dm)]
    return s, dp, qm, dm, k, v, keys


def stats_kernel(order_ref, size_ref, at_ref, kv_ref, *refs, cap, nq, tok, heads, group):
    *pieces, out_ref, x_ref, sems = refs
    low, high = head_masks(heads, 256)
    copies = load_rows(pieces, x_ref, sems)
    wide = heads * nq

    def step(i, carry):
        srcs, slots = group_of(i, group, cap, order_ref)
        s, dp, *_ = rows_of(at_ref, slots, x_ref, kv_ref, nq, tok, low, high)
        m = [jnp.max(a, axis=0, keepdims=True) for a in s]
        e = [jnp.exp(a - b) for a, b in zip(s, m)]
        for n, (a, b, c) in enumerate(zip(m, e, dp)):
            src, r = srcs[n // cap], 3 * (n % cap)
            out_ref[src, r:r + 1, 0:wide] = a
            out_ref[src, r + 1:r + 2, 0:wide] = jnp.sum(b, axis=0, keepdims=True)
            out_ref[src, r + 2:r + 3, 0:wide] = jnp.sum(b * c, axis=0, keepdims=True)
        return carry

    in_groups(order_ref, size_ref, copies, group, step)


def combine_kernel(quest_ref, st_ref, out_ref, *, cap, quests):
    ids = [quest_ref[r] for r in range(cap)]
    top = [st_ref[:, 3 * r, :] for r in range(cap)]
    size = [st_ref[:, 3 * r + 1, :] for r in range(cap)]
    mean = [st_ref[:, 3 * r + 2, :] for r in range(cap)]
    none = jnp.zeros_like(top[0])
    outs = [[none + 3e38, none, none] for _ in range(cap)]
    for j in range(quests):
        on = [ids[r] == j for r in range(cap)]
        big = functools.reduce(
            jnp.maximum,
            [jnp.max(jnp.where(on[r], top[r], -jnp.inf), axis=0, keepdims=True) for r in range(cap)],
        )
        norm, delta = 0.0, 0.0
        for r in range(cap):
            e = jnp.exp(top[r] - big)
            norm = norm + jnp.sum(jnp.where(on[r], e * size[r], 0.0), axis=0, keepdims=True)
            delta = delta + jnp.sum(jnp.where(on[r], e * mean[r], 0.0), axis=0, keepdims=True)
        inv = 1.0 / norm
        for r in range(cap):
            for i, val in enumerate((big, inv, delta * inv)):
                outs[r][i] = jnp.where(on[r], val, outs[r][i])
    for r in range(cap):
        for i in range(3):
            out_ref[:, 3 * r + i, :] = outs[r][i]


def main_kernel(
    order_ref, size_ref, at_ref, kv_ref, st_ref, x_ref, ret_ref, sum_ref, acc_ref,
    *, cap, nq, tok, heads, group, scale
):
    low, high = head_masks(heads, 256)
    acc_ref[...] = jnp.zeros_like(acc_ref)
    wide = heads * nq
    size = cap * nq

    nx, nz, nc = AXES

    def place(src):
        column = lax.div(src, nz * nc) * nc + lax.rem(src, nc)
        return pl.multiple_of((column * nz + lax.rem(lax.div(src, nc), nz)) * size, size)

    def step(i, carry):
        srcs, slots = group_of(i, group, cap, order_ref)
        s, dp, qm, dm, k, v, keys = rows_of(at_ref, slots, x_ref, kv_ref, nq, tok, low, high)
        st = [
            [st_ref[src, 3 * r + n:3 * r + n + 1, 0:wide] for n in range(3)] for src in srcs for r in range(cap)
        ]
        p = [jnp.exp(a - b[0]) * b[1] for a, b in zip(s, st)]
        w = [a.astype(BF16) for a in p]
        ds = [(a * (b - c[2])).astype(BF16) for a, b, c in zip(p, dp, st)]
        o = [gathered(dot(a, b, TN), high, nq) for a, b in zip(w, v)]
        dq = [gathered(dot(a, b, TN), low, nq) * scale for a, b in zip(ds, k)]
        dk = [dot(a, b, NN) for a, b in zip(ds, qm)]
        dv = [dot(a, b, NN) for a, b in zip(w, dm)]
        for n in range(len(slots)):
            row = pl.ds(pl.multiple_of(place(srcs[n // cap]) + n % cap * nq, nq), nq)
            ret_ref[row, 0:128] = dq[n][:, 0:128].astype(BF16)
            ret_ref[row, 128:256] = (dq[n][:, 128:256] + o[n][:, 0:128]).astype(BF16)
            ret_ref[row, 256:384] = o[n][:, 128:256].astype(BF16)
            at = pl.ds(keys[n], tok)
            acc_ref[at, 0:128] += dk[n][:, 0:128]
            acc_ref[at, 128:256] += dk[n][:, 128:256] + dv[n][:, 0:128]
            acc_ref[at, 256:384] += dv[n][:, 128:256]
        return carry

    last = (size_ref[0] + group - 1) // group
    lax.fori_loop(0, last, step, 0)

    def rest(i, carry):
        src = order_ref[i]
        ret_ref[pl.ds(place(src), size), :] = jnp.zeros((size, ret_ref.shape[1]), BF16)
        return carry

    lax.fori_loop(last * group, order_ref.shape[0], rest, 0)
    sum_ref[...] = acc_ref[...].astype(BF16)


def merge_kernel(me_ref, pick_ref, ret_ref, *out_refs):
    nz = len(out_refs)
    for s, out_ref in enumerate(out_refs):
        to = lax.rem(me_ref[0] + s, nz)
        rows = jnp.concatenate([ret_ref[u, to] for u in range(ret_ref.shape[0])], axis=0)
        out_ref[...] = dot(pick_ref[to], rows, NN).astype(BF16)


def project_kernel(shard_ref, x_ref, w_ref, *out_refs, cols):
    lane = lax.broadcasted_iota(jnp.int32, (1, 256), 1)
    grad = x_ref[:, 0:256] * (lane < cols).astype(BF16)
    mixed = x_ref[:, 128:384] * (lane >= cols - 128).astype(BF16)
    rows = x_ref.shape[0]
    many = len(out_refs)
    part = w_ref.shape[0] // many
    for s, out_ref in enumerate(out_refs):
        at = pl.ds(pl.multiple_of(lax.rem(shard_ref[0] + s, many) * part, part), part)
        out_ref[0:rows, :] = dot(mixed, w_ref[at, 128:384], NT).astype(out_ref.dtype)
        out_ref[rows:2 * rows, :] = dot(grad, w_ref[at, 0:256], NT).astype(out_ref.dtype)


def call(kernel, out_shape, ins, outs, scratch=(), mib=1):
    spaces = {"s": pltpu.SMEM, "v": pltpu.VMEM, "a": pltpu.HBM}
    out_specs = [pl.BlockSpec(memory_space=spaces[i]) for i in outs]
    return pl.pallas_call(
        kernel,
        out_shape=out_shape,
        in_specs=[pl.BlockSpec(memory_space=spaces[i]) for i in ins],
        out_specs=out_specs if len(outs) > 1 else out_specs[0],
        scratch_shapes=list(scratch),
        compiler_params=pltpu.CompilerParams(vmem_limit_bytes=mib * 1024 * 1024),
    )


def mp_hop(value, s):
    many = lax.axis_size("mp")
    return lax.ppermute(value, "mp", [(i, (i + s) % many) for i in range(many)])


def body(frames, keyframes, query_states, w_query, w_key, w_value, w_out, out_grad):
    owners = lax.axis_size("frames")
    shards = lax.axis_size("mp")
    me, shard = lax.axis_index("frames"), lax.axis_index("mp")
    fr_count, tok, width = frames.shape
    quests, keys = keyframes.shape
    nq = query_states.shape[1]
    hid = query_states.shape[2]
    cols = w_key.shape[1]
    heads = cols // HEAD_DIM
    scale = HEAD_DIM ** (-0.5)
    count = quests * keys
    cap = max(2, count // owners)
    group = 4

    queries = jnp.dot(query_states.reshape(quests * nq, hid), w_query, preferred_element_type=F32)
    d_mixed = lax.dot_general(out_grad.reshape(quests * nq, hid), w_out, NT, preferred_element_type=F32)
    local = jnp.concatenate([queries.astype(BF16) * scale, d_mixed.astype(BF16)], axis=1)
    picks = keyframes.reshape(-1)
    owner = picks >> (fr_count.bit_length() - 1)
    position = jnp.arange(count)
    same = owner[:, None] == owner[None, :]
    rank = jnp.sum(jnp.logical_and(same, position[None, :] < position[:, None]), axis=1)
    code = (picks & (fr_count - 1)) + fr_count * (position // keys) + 1
    slot = owner * cap + rank
    requests = jnp.sum(
        jnp.where(slot[None, :] == jnp.arange(owners * cap)[:, None], code[None, :], 0), axis=1
    ).astype(jnp.int32)
    asked = jnp.where(requests > 0, (requests - 1) >> (fr_count.bit_length() - 1), -1)
    quest_of = jnp.broadcast_to(asked.reshape(owners, cap).T[:, :, None], (cap, owners, 128))

    nx, nz, nc = AXES
    owners = nx * nz * nc
    bits = frames_here.bit_length() - 1
    me = me_ref[0]
    x, z, c = lax.div(me, nz * nc), lax.rem(lax.div(me, nc), nz), lax.rem(me, nc)

    def step(block, found):
        at, core, across = lax.div(block, nc * nx), lax.rem(lax.div(block, nx), nc), lax.rem(block, nx)
        away = jnp.where(lax.rem(at, 2) == 1, lax.div(at + 1, 2), nz - lax.div(at, 2))
        there = lax.rem(x - across + nx, nx) * nz + lax.rem(z - away + nz, nz)
        src = there * nc + lax.rem(c + core, nc)
        asks = (lax.rem(there, nz) * nx + lax.div(there, nz)) * nc + lax.rem(c + core, nc)
        valid = codes_ref[asks * cap] > 0
        order_ref[jnp.where(valid, found, owners - 1 - (block - found))] = src
        for r in range(cap):
            code = jnp.maximum(codes_ref[asks * cap + r] - 1, 0)
            row = (block * quests + (code >> bits)) * nq
            at_ref[src * cap + r] = jnp.where(valid, row, 0)
            at_ref[(owners + src) * cap + r] = (code & (frames_here - 1)) * tok
        return found + jnp.where(valid, 1, 0)

    near = lax.fori_loop(0, FIRST * nx * nc, step, 0)
    size_ref[1] = near
    size_ref[0] = lax.fori_loop(FIRST * nx * nc, owners, step, near)


def load_rows(pieces, x_ref, sems):
    copies, row = [], 0
    full = pieces[0].shape[0]
    for i, piece in enumerate(pieces):
        size = piece.shape[0]
        if size == full:
            row = i * full
        else:
            half, core = divmod(i - (len(pieces) - 4), 2)
            row = (len(pieces) - 4 + core) * full + half * size
        copies.append(pltpu.make_async_copy(piece, x_ref.at[pl.ds(row, size)], sems.at[i]))
        copies[-1].start()
    return copies


def in_groups(order_ref, size_ref, copies, group, step):
    early = size_ref[1] // group
    for c in copies[:2 * FIRST]:
        c.wait()
    lax.fori_loop(0, early, step, 0)
    for c in copies[2 * FIRST:]:
        c.wait()
    last = (size_ref[0] + group - 1) // group
    lax.fori_loop(early, last, step, 0)
    return last


def group_of(i, group, cap, order_ref):
    srcs = [order_ref[i * group + g] for g in range(group)]
    return srcs, [src * cap + r for src in srcs for r in range(cap)]


def rows_of(at_ref, slots, x_ref, kv_ref, nq, tok, low, high):
    at = [pl.multiple_of(at_ref[slot], nq) for slot in slots]
    keys = [pl.multiple_of(at_ref[at_ref.shape[0] // 2 + slot], tok) for slot in slots]
    qm = [spread(x_ref[pl.ds(a, nq), 0:256], low) for a in at]
    dm = [spread(x_ref[pl.ds(a, nq), 128:384], high) for a in at]
    k = [kv_ref[pl.ds(a, tok), 0:256] for a in keys]
    v = [kv_ref[pl.ds(a, tok), 128:384] for a in keys]
    s = [dot(a, b, NT) for a, b in zip(k, qm)]
    dp = [dot(a, b, NT) for a, b in zip(v, dm)]
    return s, dp, qm, dm, k, v, keys


def stats_kernel(order_ref, size_ref, at_ref, kv_ref, *refs, cap, nq, tok, heads, group):
    *pieces, out_ref, x_ref, sems = refs
    low, high = head_masks(heads, 256)
    copies = load_rows(pieces, x_ref, sems)
    wide = heads * nq

    def step(i, carry):
        srcs, slots = group_of(i, group, cap, order_ref)
        s, dp, *_ = rows_of(at_ref, slots, x_ref, kv_ref, nq, tok, low, high)
        m = [jnp.max(a, axis=0, keepdims=True) for a in s]
        e = [jnp.exp(a - b) for a, b in zip(s, m)]
        for n, (a, b, c) in enumerate(zip(m, e, dp)):
            src, r = srcs[n // cap], 3 * (n % cap)
            out_ref[src, r:r + 1, 0:wide] = a
            out_ref[src, r + 1:r + 2, 0:wide] = jnp.sum(b, axis=0, keepdims=True)
            out_ref[src, r + 2:r + 3, 0:wide] = jnp.sum(b * c, axis=0, keepdims=True)
        return carry

    in_groups(order_ref, size_ref, copies, group, step)


def combine_kernel(quest_ref, st_ref, out_ref, *, cap, quests):
    ids = [quest_ref[r] for r in range(cap)]
    top = [st_ref[:, 3 * r, :] for r in range(cap)]
    size = [st_ref[:, 3 * r + 1, :] for r in range(cap)]
    mean = [st_ref[:, 3 * r + 2, :] for r in range(cap)]
    none = jnp.zeros_like(top[0])
    outs = [[none + 3e38, none, none] for _ in range(cap)]
    for j in range(quests):
        on = [ids[r] == j for r in range(cap)]
        big = functools.reduce(
            jnp.maximum,
            [jnp.max(jnp.where(on[r], top[r], -jnp.inf), axis=0, keepdims=True) for r in range(cap)],
        )
        norm, delta = 0.0, 0.0
        for r in range(cap):
            e = jnp.exp(top[r] - big)
            norm = norm + jnp.sum(jnp.where(on[r], e * size[r], 0.0), axis=0, keepdims=True)
            delta = delta + jnp.sum(jnp.where(on[r], e * mean[r], 0.0), axis=0, keepdims=True)
        inv = 1.0 / norm
        for r in range(cap):
            for i, val in enumerate((big, inv, delta * inv)):
                outs[r][i] = jnp.where(on[r], val, outs[r][i])
    for r in range(cap):
        for i in range(3):
            out_ref[:, 3 * r + i, :] = outs[r][i]


def main_kernel(
    order_ref, size_ref, at_ref, kv_ref, st_ref, x_ref, ret_ref, sum_ref, acc_ref,
    *, cap, nq, tok, heads, group, scale
):
    low, high = head_masks(heads, 256)
    acc_ref[...] = jnp.zeros_like(acc_ref)
    wide = heads * nq
    size = cap * nq

    nx, nz, nc = AXES

    def place(src):
        column = lax.div(src, nz * nc) * nc + lax.rem(src, nc)
        return pl.multiple_of((column * nz + lax.rem(lax.div(src, nc), nz)) * size, size)

    def step(i, carry):
        srcs, slots = group_of(i, group, cap, order_ref)
        s, dp, qm, dm, k, v, keys = rows_of(at_ref, slots, x_ref, kv_ref, nq, tok, low, high)
        st = [
            [st_ref[src, 3 * r + n:3 * r + n + 1, 0:wide] for n in range(3)] for src in srcs for r in range(cap)
        ]
        p = [jnp.exp(a - b[0]) * b[1] for a, b in zip(s, st)]
        w = [a.astype(BF16) for a in p]
        ds = [(a * (b - c[2])).astype(BF16) for a, b, c in zip(p, dp, st)]
        o = [gathered(dot(a, b, TN), high, nq) for a, b in zip(w, v)]
        dq = [gathered(dot(a, b, TN), low, nq) * scale for a, b in zip(ds, k)]
        dk = [dot(a, b, NN) for a, b in zip(ds, qm)]
        dv = [dot(a, b, NN) for a, b in zip(w, dm)]
        for n in range(len(slots)):
            row = pl.ds(pl.multiple_of(place(srcs[n // cap]) + n % cap * nq, nq), nq)
            ret_ref[row, 0:128] = dq[n][:, 0:128].astype(BF16)
            ret_ref[row, 128:256] = (dq[n][:, 128:256] + o[n][:, 0:128]).astype(BF16)
            ret_ref[row, 256:384] = o[n][:, 128:256].astype(BF16)
            at = pl.ds(keys[n], tok)
            acc_ref[at, 0:128] += dk[n][:, 0:128]
            acc_ref[at, 128:256] += dk[n][:, 128:256] + dv[n][:, 0:128]
            acc_ref[at, 256:384] += dv[n][:, 128:256]
        return carry

    last = (size_ref[0] + group - 1) // group
    lax.fori_loop(0, last, step, 0)

    def rest(i, carry):
        src = order_ref[i]
        ret_ref[pl.ds(place(src), size), :] = jnp.zeros((size, ret_ref.shape[1]), BF16)
        return carry

    lax.fori_loop(last * group, order_ref.shape[0], rest, 0)
    sum_ref[...] = acc_ref[...].astype(BF16)


def merge_kernel(me_ref, pick_ref, ret_ref, *out_refs):
    nz = len(out_refs)
    for s, out_ref in enumerate(out_refs):
        to = lax.rem(me_ref[0] + s, nz)
        rows = jnp.concatenate([ret_ref[u, to] for u in range(ret_ref.shape[0])], axis=0)
        out_ref[...] = dot(pick_ref[to], rows, NN).astype(BF16)


def finish_kernel(*refs, cols):
    *ins, att_ref, grad_ref = refs
    many = len(ins) // 2
    lane = lax.broadcasted_iota(jnp.int32, (1, 256), 1)
    low = (lane < cols).astype(BF16)
    high = (lane >= cols - 128).astype(BF16)
    att, grad = 0.0, 0.0
    for x_ref, w_ref in zip(ins[:many], ins[many:]):
        grad = grad + dot(x_ref[:, 0:256] * low, w_ref[:, 0:256], NT)
        att = att + dot(x_ref[:, 128:384] * high, w_ref[:, 128:384], NT)
    att_ref[...] = att.astype(BF16)
    grad_ref[...] = grad.astype(BF16)


def call(kernel, out_shape, ins, outs, scratch=(), mib=1):
    spaces = {"s": pltpu.SMEM, "v": pltpu.VMEM, "a": pltpu.HBM}
    out_specs = [pl.BlockSpec(memory_space=spaces[i]) for i in outs]
    return pl.pallas_call(
        kernel,
        out_shape=out_shape,
        in_specs=[pl.BlockSpec(memory_space=spaces[i]) for i in ins],
        out_specs=out_specs if len(outs) > 1 else out_specs[0],
        scratch_shapes=list(scratch),
        compiler_params=pltpu.CompilerParams(vmem_limit_bytes=mib * 1024 * 1024),
    )


def mp_hop(value, s):
    many = lax.axis_size("mp")
    return lax.ppermute(value, "mp", [(i, (i + s) % many) for i in range(many)])


def body(frames, keyframes, query_states, w_query, w_key, w_value, w_out, out_grad):
    owners = lax.axis_size("frames")
    shards = lax.axis_size("mp")
    me, shard = lax.axis_index("frames"), lax.axis_index("mp")
    fr_count, tok, width = frames.shape
    quests, keys = keyframes.shape
    nq = query_states.shape[1]
    hid = query_states.shape[2]
    cols = w_key.shape[1]
    heads = cols // HEAD_DIM
    scale = HEAD_DIM ** (-0.5)
    count = quests * keys
    cap = max(2, count // owners)
    group = 4

    queries = jnp.dot(query_states.reshape(quests * nq, hid), w_query, preferred_element_type=F32)
    d_mixed = lax.dot_general(out_grad.reshape(quests * nq, hid), w_out, NT, preferred_element_type=F32)
    local = jnp.concatenate([queries.astype(BF16) * scale, d_mixed.astype(BF16)], axis=1)
    picks = keyframes.reshape(-1)
    owner = picks >> (fr_count.bit_length() - 1)
    position = jnp.arange(count)
    same = owner[:, None] == owner[None, :]
    rank = jnp.sum(jnp.logical_and(same, position[None, :] < position[:, None]), axis=1)
    code = (picks & (fr_count - 1)) + fr_count * (position // keys) + 1
    slot = owner * cap + rank
    requests = jnp.sum(
        jnp.where(slot[None, :] == jnp.arange(owners * cap)[:, None], code[None, :], 0), axis=1
    ).astype(jnp.int32)
    asked = jnp.where(requests > 0, (requests - 1) >> (fr_count.bit_length() - 1), -1)
    quest_of = jnp.broadcast_to(asked.reshape(owners, cap).T[:, :, None], (cap, owners, 128))
    put = jnp.arange(quests * nq)[:, None]
    take = jnp.arange(owners * cap * nq)[None, :]
    pick_sum = jnp.logical_and(put // nq == jnp.repeat(asked, nq)[None, :], put % nq == take % nq).astype(BF16)

    w_both = jnp.concatenate([w_key, w_value], axis=1)
    bank = jnp.dot(frames.reshape(fr_count * tok, width), w_both, preferred_element_type=F32).astype(BF16)
    flat, line = planes()
    nx, nz, nc = AXES
    mine = jnp.concatenate([local] + [hop(local, dx=s) for s in range(1, nx)], axis=0)
    passed = requests.reshape(nx, nz, nc, cap).swapaxes(0, 1).reshape(nz, nx * nc * cap)
    passed = lax.all_to_all(passed, "frames", 0, 0, axis_index_groups=line, tiled=True)
    mine, passed, bank = lax.optimization_barrier((mine, passed, bank))
    incoming = passed.reshape(nz, nx * nc, cap).swapaxes(0, 1).reshape(nx * nc, nz * cap)
    incoming = lax.all_to_all(incoming, "frames", 0, 0, axis_index_groups=flat, tiled=True)
    incoming = incoming.reshape(nx * nc, nz, cap).swapaxes(0, 1).reshape(-1)
    ways = [(mine, mine)]
    ways.append((hop(ways[-1][0], dz=1), hop(ways[-1][1], dz=-1)))
    ways[-1], incoming = lax.optimization_barrier((ways[-1], incoming))
    ints = lambda *shape: jax.ShapeDtypeStruct(shape, jnp.int32)
    order, sizes, at = call(
        functools.partial(plan_kernel, cap=cap, quests=quests, nq=nq, tok=tok, frames_here=fr_count),
        (ints(owners), ints(2), ints(2 * owners * cap)),
        "ss",
        "sss",
    )(incoming, me.astype(jnp.int32).reshape(1))
    ways.append((hop(ways[-1][0], dz=1), hop(ways[-1][1], dz=-1)))
    ways[-1], order, sizes, at, quest_of = lax.optimization_barrier((ways[-1], order, sizes, at, quest_of))
    ways.append((hop(ways[-1][0], dz=1), hop(ways[-1][1], dz=-1)))
    half = mine.shape[0] // 2
    pieces = [mine] + [way for pair in ways[1:] for way in pair]
    pieces += [hop(ways[-1][0][:half], dz=1), hop(ways[-1][1][half:], dz=-1)]
    pieces = [p for piece in pieces for p in (piece, hop(piece, dc=1))]

    dims = dict(cap=cap, nq=nq, tok=tok, heads=heads, group=group)
    held = (owners * cap * nq, 2 * cols)
    stat_shape = jax.ShapeDtypeStruct((owners, 8, 128), F32)
    rows = jax.ShapeDtypeStruct((owners * quests * nq, 2 * cols), BF16)
    stats, rows = call(
        functools.partial(stats_kernel, **dims),
        (stat_shape, rows),
        "sssv" + "a" * len(pieces),
        "vv",
        [pltpu.SemaphoreType.DMA((len(pieces),))],
        4,
    )(order, sizes, at, bank, *pieces)
    stats = lax.all_to_all(stats, "frames", split_axis=0, concat_axis=0, tiled=True)
    stats = call(functools.partial(combine_kernel, cap=cap, quests=quests), stat_shape, "vv", "v")(quest_of, stats)
    stats = lax.all_to_all(stats, "frames", split_axis=0, concat_axis=0, tiled=True)
    partial, sums = call(
        functools.partial(main_kernel, scale=scale, **dims),
        (jax.ShapeDtypeStruct(held, BF16), jax.ShapeDtypeStruct((fr_count * tok, 2 * cols), BF16)),
        "sssvvv",
        "vv",
        [pltpu.VMEM((fr_count * tok, 2 * cols), F32)],
        8,
    )(order, sizes, at, bank, stats, rows)
    partial = lax.all_to_all(
        partial.reshape(nx * nc, nz * cap * nq, 2 * cols), "frames", 0, 0, axis_index_groups=flat, tiled=True
    ).reshape(nx * nc, nz, cap * nq, 2 * cols)
    asked = jnp.where(passed > 0, (passed - 1) >> (fr_count.bit_length() - 1), -1)
    put = jnp.arange(quests * nq)[None, :, None]
    take = jnp.arange(nx * nc * cap * nq)[None, None, :]
    asked = jnp.repeat(asked.reshape(nz, 1, nx * nc * cap), nq, axis=2)
    pick_sum = jnp.logical_and(put // nq == asked, put % nq == take % nq).astype(BF16)

    w_q_out = jnp.concatenate([w_query, w_out.T], axis=1)
    own = [(shard + s) % shards for s in range(shards)]
    part = hid // shards
    slab = width // shards
    terms = [
        lax.dot_general(
            sums, lax.dynamic_slice_in_dim(w_both, own[s] * slab, slab, 0), NT, preferred_element_type=F32
        )
        for s in range(shards)
    ]
    frame_grad = terms[0]
    for s in range(1, shards):
        frame_grad = frame_grad + mp_hop(terms[s].astype(BF16), s).astype(F32)

    frame_grad = frame_grad.astype(BF16).reshape(fr_count, tok, slab)
    partial, w_q_out, pick_sum = lax.optimization_barrier((partial, w_q_out, pick_sum))
    mine_shape = jax.ShapeDtypeStruct((quests * nq, 2 * cols), BF16)
    merged = call(merge_kernel, (mine_shape,) * nz, "svv", "v" * nz, mib=4)(
        lax.rem(lax.div(me, nc), nz).astype(jnp.int32).reshape(1), pick_sum, partial
    )
    mine = merged[0].astype(F32)
    for s in range(1, nz):
        mine = mine + hop(merged[s], dz=s).astype(F32)
    mine, frame_grad = lax.optimization_barrier((mine.astype(BF16), frame_grad))
    block = lambda kind: jax.ShapeDtypeStruct((2 * quests * nq, part), kind)
    blocks = call(
        functools.partial(project_kernel, cols=cols),
        (block(F32),) + (block(BF16),) * (shards - 1),
        "svv",
        "v" * shards,
        mib=2,
    )(shard.astype(jnp.int32).reshape(1), mine, w_q_out)
    both = blocks[0]
    for s in range(1, shards):
        both = both + mp_hop(blocks[s], s).astype(F32)
    both = both.astype(BF16).reshape(2, quests, nq, part)
    return both[0], both[1], frame_grad


def solution(mesh):
    placed = (
        P("frames", None, None),
        P("frames", None),
        P("frames", None, None),
        P(None, "mp"),
        P(None, "mp"),
        P(None, "mp"),
        P("mp", None),
        P("frames", None, None),
    )
    return jax.shard_map(
        body,
        mesh=mesh,
        in_specs=placed,
        out_specs=(P("frames", None, "mp"), P("frames", None, "mp"), P("frames", None, "mp")),
        check_vma=False,
    )
```

```python
import functools

import jax
import jax.numpy as jnp
from jax import lax
from jax.experimental import pallas as pl
from jax.experimental.pallas import tpu as pltpu
from jax.sharding import PartitionSpec as P

HEAD_DIM = 64
NT = (((1,), (1,)), ((), ()))
TN = (((0,), (0,)), ((), ()))
NN = (((1,), (0,)), ((), ()))
F32 = jnp.float32
BF16 = jnp.bfloat16


def dot(a, b, dims):
    return lax.dot_general(a, b, dims, preferred_element_type=F32)


def head_masks(heads, wide):
    lane = lax.broadcasted_iota(jnp.int32, (1, wide), 1) // HEAD_DIM
    low = [(lane == h).astype(BF16) for h in range(heads)]
    high = [(lane == h + 1).astype(BF16) for h in range(heads)]
    return low, high


def spread(block, masks):
    return jnp.concatenate([block * m for m in masks], axis=0)


def gathered(block, masks, nq):
    total = block[:nq] * masks[0].astype(F32)
    for h in range(1, len(masks)):
        total = total + block[h * nq:(h + 1) * nq] * masks[h].astype(F32)
    return total


AXES = (4, 8, 2)
FIRST = 3


def frames_perm(dx=0, dz=0, dc=0):
    nx, nz, nc = AXES
    pairs = []
    for x in range(nx):
        for z in range(nz):
            for c in range(nc):
                to = (((x + dx) % nx) * nz + (z + dz) % nz) * nc + (c + dc) % nc
                pairs.append(((x * nz + z) * nc + c, to))
    return pairs


def planes():
    nx, nz, nc = AXES
    number = lambda x, z, c: (x * nz + z) * nc + c
    flat = [[number(x, z, c) for x in range(nx) for c in range(nc)] for z in range(nz)]
    line = [[number(x, z, c) for z in range(nz)] for x in range(nx) for c in range(nc)]
    return flat, line


def hop(value, **shift):
    return lax.ppermute(value, "frames", frames_perm(**shift))


def plan_kernel(codes_ref, me_ref, order_ref, size_ref, at_ref, *, cap, quests, nq, tok, frames_here):
    nx, nz, nc = AXES
    owners = nx * nz * nc
    bits = frames_here.bit_length() - 1
    me = me_ref[0]
    x, z, c = lax.div(me, nz * nc), lax.rem(lax.div(me, nc), nz), lax.rem(me, nc)

    def step(block, found):
        at, core, across = lax.div(block, nc * nx), lax.rem(lax.div(block, nx), nc), lax.rem(block, nx)
        away = jnp.where(lax.rem(at, 2) == 1, lax.div(at + 1, 2), nz - lax.div(at, 2))
        there = lax.rem(x - across + nx, nx) * nz + lax.rem(z - away + nz, nz)
        src = there * nc + lax.rem(c + core, nc)
        asks = (lax.rem(there, nz) * nx + lax.div(there, nz)) * nc + lax.rem(c + core, nc)
        valid = codes_ref[asks * cap] > 0
        order_ref[jnp.where(valid, found, owners - 1 - (block - found))] = src
        for r in range(cap):
            code = jnp.maximum(codes_ref[asks * cap + r] - 1, 0)
            row = (block * quests + (code >> bits)) * nq
            at_ref[src * cap + r] = jnp.where(valid, row, 0)
            at_ref[(owners + src) * cap + r] = (code & (frames_here - 1)) * tok
        return found + jnp.where(valid, 1, 0)

    near = lax.fori_loop(0, FIRST * nx * nc, step, 0)
    size_ref[1] = near
    size_ref[0] = lax.fori_loop(FIRST * nx * nc, owners, step, near)


def load_rows(pieces, x_ref, sems):
    copies, row = [], 0
    full = pieces[0].shape[0]
    for i, piece in enumerate(pieces):
        size = piece.shape[0]
        if size == full:
            row = i * full
        else:
            half, core = divmod(i - (len(pieces) - 4), 2)
            row = (len(pieces) - 4 + core) * full + half * size
        copies.append(pltpu.make_async_copy(piece, x_ref.at[pl.ds(row, size)], sems.at[i]))
        copies[-1].start()
    return copies


def in_groups(order_ref, size_ref, copies, group, step):
    early = size_ref[1] // group
    for c in copies[:2 * FIRST]:
        c.wait()
    lax.fori_loop(0, early, step, 0)
    for c in copies[2 * FIRST:]:
        c.wait()
    last = (size_ref[0] + group - 1) // group
    lax.fori_loop(early, last, step, 0)
    return last


def group_of(i, group, cap, order_ref):
    srcs = [order_ref[i * group + g] for g in range(group)]
    return srcs, [src * cap + r for src in srcs for r in range(cap)]


def rows_of(at_ref, slots, x_ref, kv_ref, nq, tok, low, high):
    at = [pl.multiple_of(at_ref[slot], nq) for slot in slots]
    keys = [pl.multiple_of(at_ref[at_ref.shape[0] // 2 + slot], tok) for slot in slots]
    qm = [spread(x_ref[pl.ds(a, nq), 0:256], low) for a in at]
    dm = [spread(x_ref[pl.ds(a, nq), 128:384], high) for a in at]
    k = [kv_ref[pl.ds(a, tok), 0:256] for a in keys]
    v = [kv_ref[pl.ds(a, tok), 128:384] for a in keys]
    s = [dot(a, b, NT) for a, b in zip(k, qm)]
    dp = [dot(a, b, NT) for a, b in zip(v, dm)]
    return s, dp, qm, dm, k, v, keys


def stats_kernel(order_ref, size_ref, at_ref, kv_ref, *refs, cap, nq, tok, heads, group):
    *pieces, out_ref, x_ref, sems = refs
    low, high = head_masks(heads, 256)
    copies = load_rows(pieces, x_ref, sems)
    wide = heads * nq

    def step(i, carry):
        srcs, slots = group_of(i, group, cap, order_ref)
        s, dp, *_ = rows_of(at_ref, slots, x_ref, kv_ref, nq, tok, low, high)
        m = [jnp.max(a, axis=0, keepdims=True) for a in s]
        e = [jnp.exp(a - b) for a, b in zip(s, m)]
        for n, (a, b, c) in enumerate(zip(m, e, dp)):
            src, r = srcs[n // cap], 3 * (n % cap)
            out_ref[src, r:r + 1, 0:wide] = a
            out_ref[src, r + 1:r + 2, 0:wide] = jnp.sum(b, axis=0, keepdims=True)
            out_ref[src, r + 2:r + 3, 0:wide] = jnp.sum(b * c, axis=0, keepdims=True)
        return carry

    in_groups(order_ref, size_ref, copies, group, step)


def combine_kernel(quest_ref, st_ref, out_ref, *, cap, quests):
    ids = [quest_ref[r] for r in range(cap)]
    top = [st_ref[:, 3 * r, :] for r in range(cap)]
    size = [st_ref[:, 3 * r + 1, :] for r in range(cap)]
    mean = [st_ref[:, 3 * r + 2, :] for r in range(cap)]
    none = jnp.zeros_like(top[0])
    outs = [[none + 3e38, none, none] for _ in range(cap)]
    for j in range(quests):
        on = [ids[r] == j for r in range(cap)]
        big = functools.reduce(
            jnp.maximum,
            [jnp.max(jnp.where(on[r], top[r], -jnp.inf), axis=0, keepdims=True) for r in range(cap)],
        )
        norm, delta = 0.0, 0.0
        for r in range(cap):
            e = jnp.exp(top[r] - big)
            norm = norm + jnp.sum(jnp.where(on[r], e * size[r], 0.0), axis=0, keepdims=True)
            delta = delta + jnp.sum(jnp.where(on[r], e * mean[r], 0.0), axis=0, keepdims=True)
        inv = 1.0 / norm
        for r in range(cap):
            for i, val in enumerate((big, inv, delta * inv)):
                outs[r][i] = jnp.where(on[r], val, outs[r][i])
    for r in range(cap):
        for i in range(3):
            out_ref[:, 3 * r + i, :] = outs[r][i]


def main_kernel(
    order_ref, size_ref, at_ref, kv_ref, st_ref, x_ref, ret_ref, sum_ref, acc_ref,
    *, cap, nq, tok, heads, group, scale
):
    low, high = head_masks(heads, 256)
    acc_ref[...] = jnp.zeros_like(acc_ref)
    wide = heads * nq
    size = cap * nq

    nx, nz, nc = AXES

    def place(src):
        column = lax.div(src, nz * nc) * nc + lax.rem(src, nc)
        return pl.multiple_of((column * nz + lax.rem(lax.div(src, nc), nz)) * size, size)

    def step(i, carry):
        srcs, slots = group_of(i, group, cap, order_ref)
        s, dp, qm, dm, k, v, keys = rows_of(at_ref, slots, x_ref, kv_ref, nq, tok, low, high)
        st = [
            [st_ref[src, 3 * r + n:3 * r + n + 1, 0:wide] for n in range(3)] for src in srcs for r in range(cap)
        ]
        p = [jnp.exp(a - b[0]) * b[1] for a, b in zip(s, st)]
        w = [a.astype(BF16) for a in p]
        ds = [(a * (b - c[2])).astype(BF16) for a, b, c in zip(p, dp, st)]
        o = [gathered(dot(a, b, TN), high, nq) for a, b in zip(w, v)]
        dq = [gathered(dot(a, b, TN), low, nq) * scale for a, b in zip(ds, k)]
        dk = [dot(a, b, NN) for a, b in zip(ds, qm)]
        dv = [dot(a, b, NN) for a, b in zip(w, dm)]
        for n in range(len(slots)):
            row = pl.ds(pl.multiple_of(place(srcs[n // cap]) + n % cap * nq, nq), nq)
            ret_ref[row, 0:128] = dq[n][:, 0:128].astype(BF16)
            ret_ref[row, 128:256] = (dq[n][:, 128:256] + o[n][:, 0:128]).astype(BF16)
            ret_ref[row, 256:384] = o[n][:, 128:256].astype(BF16)
            at = pl.ds(keys[n], tok)
            acc_ref[at, 0:128] += dk[n][:, 0:128]
            acc_ref[at, 128:256] += dk[n][:, 128:256] + dv[n][:, 0:128]
            acc_ref[at, 256:384] += dv[n][:, 128:256]
        return carry

    last = (size_ref[0] + group - 1) // group
    lax.fori_loop(0, last, step, 0)

    def rest(i, carry):
        src = order_ref[i]
        ret_ref[pl.ds(place(src), size), :] = jnp.zeros((size, ret_ref.shape[1]), BF16)
        return carry

    lax.fori_loop(last * group, order_ref.shape[0], rest, 0)
    sum_ref[...] = acc_ref[...].astype(BF16)


def merge_kernel(me_ref, pick_ref, ret_ref, *out_refs):
    nz = len(out_refs)
    for s, out_ref in enumerate(out_refs):
        to = lax.rem(me_ref[0] + s, nz)
        rows = jnp.concatenate([ret_ref[u, to] for u in range(ret_ref.shape[0])], axis=0)
        out_ref[...] = dot(pick_ref[to], rows, NN).astype(BF16)


def project_kernel(*refs, cols):
    lane = lax.broadcasted_iota(jnp.int32, (1, 256), 1)
    *parts, w_ref, out_ref = refs
    total = parts[0][...].astype(F32)
    for part_ref in parts[1:]:
        total = total + part_ref[...].astype(F32)
    total = total.astype(BF16)
    grad = total[:, 0:256] * (lane < cols).astype(BF16)
    mixed = total[:, 128:384] * (lane >= cols - 128).astype(BF16)
    rows = total.shape[0]
    many = out_ref.shape[0]
    part = w_ref.shape[0] // many
    for to in range(many):
        at = pl.ds(to * part, part)
        out_ref[to, 0:rows, :] = dot(mixed, w_ref[at, 128:384], NT).astype(out_ref.dtype)
        out_ref[to, rows:2 * rows, :] = dot(grad, w_ref[at, 0:256], NT).astype(out_ref.dtype)


def add_kernel(blocks_ref, att_ref, grad_ref):
    rows = att_ref.shape[0]
    for at, out_ref in ((0, att_ref), (rows, grad_ref)):
        total = blocks_ref[0, at:at + rows, :].astype(F32)
        for i in range(1, blocks_ref.shape[0]):
            total = total + blocks_ref[i, at:at + rows, :].astype(F32)
        out_ref[...] = total.astype(out_ref.dtype)


def call(kernel, out_shape, ins, outs, scratch=(), mib=1):
    spaces = {"s": pltpu.SMEM, "v": pltpu.VMEM, "a": pltpu.HBM}
    out_specs = [pl.BlockSpec(memory_space=spaces[i]) for i in outs]
    return pl.pallas_call(
        kernel,
        out_shape=out_shape,
        in_specs=[pl.BlockSpec(memory_space=spaces[i]) for i in ins],
        out_specs=out_specs if len(outs) > 1 else out_specs[0],
        scratch_shapes=list(scratch),
        compiler_params=pltpu.CompilerParams(vmem_limit_bytes=mib * 1024 * 1024),
    )


def mp_hop(value, s):
    many = lax.axis_size("mp")
    return lax.ppermute(value, "mp", [(i, (i + s) % many) for i in range(many)])


def body(frames, keyframes, query_states, w_query, w_key, w_value, w_out, out_grad):
    owners = lax.axis_size("frames")
    shards = lax.axis_size("mp")
    me, shard = lax.axis_index("frames"), lax.axis_index("mp")
    fr_count, tok, width = frames.shape
    quests, keys = keyframes.shape
    nq = query_states.shape[1]
    hid = query_states.shape[2]
    cols = w_key.shape[1]
    heads = cols // HEAD_DIM
    scale = HEAD_DIM ** (-0.5)
    count = quests * keys
    cap = max(2, count // owners)
    group = 4

    queries = jnp.dot(query_states.reshape(quests * nq, hid), w_query, preferred_element_type=F32)
    d_mixed = lax.dot_general(out_grad.reshape(quests * nq, hid), w_out, NT, preferred_element_type=F32)
    local = jnp.concatenate([queries.astype(BF16) * scale, d_mixed.astype(BF16)], axis=1)
    picks = keyframes.reshape(-1)
    owner = picks >> (fr_count.bit_length() - 1)
    position = jnp.arange(count)
    same = owner[:, None] == owner[None, :]
    rank = jnp.sum(jnp.logical_and(same, position[None, :] < position[:, None]), axis=1)
    code = (picks & (fr_count - 1)) + fr_count * (position // keys) + 1
    slot = owner * cap + rank
    requests = jnp.sum(
        jnp.where(slot[None, :] == jnp.arange(owners * cap)[:, None], code[None, :], 0), axis=1
    ).astype(jnp.int32)
    asked = jnp.where(requests > 0, (requests - 1) >> (fr_count.bit_length() - 1), -1)
    quest_of = jnp.broadcast_to(asked.reshape(owners, cap).T[:, :, None], (cap, owners, 128))

    nx, nz, nc = AXES
    owners = nx * nz * nc
    bits = frames_here.bit_length() - 1
    me = me_ref[0]
    x, z, c = lax.div(me, nz * nc), lax.rem(lax.div(me, nc), nz), lax.rem(me, nc)

    def step(block, found):
        at, core, across = lax.div(block, nc * nx), lax.rem(lax.div(block, nx), nc), lax.rem(block, nx)
        away = jnp.where(lax.rem(at, 2) == 1, lax.div(at + 1, 2), nz - lax.div(at, 2))
        there = lax.rem(x - across + nx, nx) * nz + lax.rem(z - away + nz, nz)
        src = there * nc + lax.rem(c + core, nc)
        asks = (lax.rem(there, nz) * nx + lax.div(there, nz)) * nc + lax.rem(c + core, nc)
        valid = codes_ref[asks * cap] > 0
        order_ref[jnp.where(valid, found, owners - 1 - (block - found))] = src
        for r in range(cap):
            code = jnp.maximum(codes_ref[asks * cap + r] - 1, 0)
            row = (block * quests + (code >> bits)) * nq
            at_ref[src * cap + r] = jnp.where(valid, row, 0)
            at_ref[(owners + src) * cap + r] = (code & (frames_here - 1)) * tok
        return found + jnp.where(valid, 1, 0)

    near = lax.fori_loop(0, FIRST * nx * nc, step, 0)
    size_ref[1] = near
    size_ref[0] = lax.fori_loop(FIRST * nx * nc, owners, step, near)


def load_rows(pieces, x_ref, sems):
    copies, row = [], 0
    full = pieces[0].shape[0]
    for i, piece in enumerate(pieces):
        size = piece.shape[0]
        if size == full:
            row = i * full
        else:
            half, core = divmod(i - (len(pieces) - 4), 2)
            row = (len(pieces) - 4 + core) * full + half * size
        copies.append(pltpu.make_async_copy(piece, x_ref.at[pl.ds(row, size)], sems.at[i]))
        copies[-1].start()
    return copies


def in_groups(order_ref, size_ref, copies, group, step):
    early = size_ref[1] // group
    for c in copies[:2 * FIRST]:
        c.wait()
    lax.fori_loop(0, early, step, 0)
    for c in copies[2 * FIRST:]:
        c.wait()
    last = (size_ref[0] + group - 1) // group
    lax.fori_loop(early, last, step, 0)
    return last


def group_of(i, group, cap, order_ref):
    srcs = [order_ref[i * group + g] for g in range(group)]
    return srcs, [src * cap + r for src in srcs for r in range(cap)]


def rows_of(at_ref, slots, x_ref, kv_ref, nq, tok, low, high):
    at = [pl.multiple_of(at_ref[slot], nq) for slot in slots]
    keys = [pl.multiple_of(at_ref[at_ref.shape[0] // 2 + slot], tok) for slot in slots]
    qm = [spread(x_ref[pl.ds(a, nq), 0:256], low) for a in at]
    dm = [spread(x_ref[pl.ds(a, nq), 128:384], high) for a in at]
    k = [kv_ref[pl.ds(a, tok), 0:256] for a in keys]
    v = [kv_ref[pl.ds(a, tok), 128:384] for a in keys]
    s = [dot(a, b, NT) for a, b in zip(k, qm)]
    dp = [dot(a, b, NT) for a, b in zip(v, dm)]
    return s, dp, qm, dm, k, v, keys


def stats_kernel(order_ref, size_ref, at_ref, kv_ref, *refs, cap, nq, tok, heads, group):
    *pieces, out_ref, x_ref, sems = refs
    low, high = head_masks(heads, 256)
    copies = load_rows(pieces, x_ref, sems)
    wide = heads * nq

    def step(i, carry):
        srcs, slots = group_of(i, group, cap, order_ref)
        s, dp, *_ = rows_of(at_ref, slots, x_ref, kv_ref, nq, tok, low, high)
        m = [jnp.max(a, axis=0, keepdims=True) for a in s]
        e = [jnp.exp(a - b) for a, b in zip(s, m)]
        for n, (a, b, c) in enumerate(zip(m, e, dp)):
            src, r = srcs[n // cap], 3 * (n % cap)
            out_ref[src, r:r + 1, 0:wide] = a
            out_ref[src, r + 1:r + 2, 0:wide] = jnp.sum(b, axis=0, keepdims=True)
            out_ref[src, r + 2:r + 3, 0:wide] = jnp.sum(b * c, axis=0, keepdims=True)
        return carry

    in_groups(order_ref, size_ref, copies, group, step)


def combine_kernel(quest_ref, st_ref, out_ref, *, cap, quests):
    ids = [quest_ref[r] for r in range(cap)]
    top = [st_ref[:, 3 * r, :] for r in range(cap)]
    size = [st_ref[:, 3 * r + 1, :] for r in range(cap)]
    mean = [st_ref[:, 3 * r + 2, :] for r in range(cap)]
    none = jnp.zeros_like(top[0])
    outs = [[none + 3e38, none, none] for _ in range(cap)]
    for j in range(quests):
        on = [ids[r] == j for r in range(cap)]
        big = functools.reduce(
            jnp.maximum,
            [jnp.max(jnp.where(on[r], top[r], -jnp.inf), axis=0, keepdims=True) for r in range(cap)],
        )
        norm, delta = 0.0, 0.0
        for r in range(cap):
            e = jnp.exp(top[r] - big)
            norm = norm + jnp.sum(jnp.where(on[r], e * size[r], 0.0), axis=0, keepdims=True)
            delta = delta + jnp.sum(jnp.where(on[r], e * mean[r], 0.0), axis=0, keepdims=True)
        inv = 1.0 / norm
        for r in range(cap):
            for i, val in enumerate((big, inv, delta * inv)):
                outs[r][i] = jnp.where(on[r], val, outs[r][i])
    for r in range(cap):
        for i in range(3):
            out_ref[:, 3 * r + i, :] = outs[r][i]


def main_kernel(
    order_ref, size_ref, at_ref, kv_ref, st_ref, x_ref, ret_ref, sum_ref, acc_ref,
    *, cap, nq, tok, heads, group, scale
):
    low, high = head_masks(heads, 256)
    acc_ref[...] = jnp.zeros_like(acc_ref)
    wide = heads * nq
    size = cap * nq

    nx, nz, nc = AXES

    def place(src):
        column = lax.div(src, nz * nc) * nc + lax.rem(src, nc)
        return pl.multiple_of((column * nz + lax.rem(lax.div(src, nc), nz)) * size, size)

    def step(i, carry):
        srcs, slots = group_of(i, group, cap, order_ref)
        s, dp, qm, dm, k, v, keys = rows_of(at_ref, slots, x_ref, kv_ref, nq, tok, low, high)
        st = [
            [st_ref[src, 3 * r + n:3 * r + n + 1, 0:wide] for n in range(3)] for src in srcs for r in range(cap)
        ]
        p = [jnp.exp(a - b[0]) * b[1] for a, b in zip(s, st)]
        w = [a.astype(BF16) for a in p]
        ds = [(a * (b - c[2])).astype(BF16) for a, b, c in zip(p, dp, st)]
        o = [gathered(dot(a, b, TN), high, nq) for a, b in zip(w, v)]
        dq = [gathered(dot(a, b, TN), low, nq) * scale for a, b in zip(ds, k)]
        dk = [dot(a, b, NN) for a, b in zip(ds, qm)]
        dv = [dot(a, b, NN) for a, b in zip(w, dm)]
        for n in range(len(slots)):
            row = pl.ds(pl.multiple_of(place(srcs[n // cap]) + n % cap * nq, nq), nq)
            ret_ref[row, 0:128] = dq[n][:, 0:128].astype(BF16)
            ret_ref[row, 128:256] = (dq[n][:, 128:256] + o[n][:, 0:128]).astype(BF16)
            ret_ref[row, 256:384] = o[n][:, 128:256].astype(BF16)
            at = pl.ds(keys[n], tok)
            acc_ref[at, 0:128] += dk[n][:, 0:128]
            acc_ref[at, 128:256] += dk[n][:, 128:256] + dv[n][:, 0:128]
            acc_ref[at, 256:384] += dv[n][:, 128:256]
        return carry

    last = (size_ref[0] + group - 1) // group
    lax.fori_loop(0, last, step, 0)

    def rest(i, carry):
        src = order_ref[i]
        ret_ref[pl.ds(place(src), size), :] = jnp.zeros((size, ret_ref.shape[1]), BF16)
        return carry

    lax.fori_loop(last * group, order_ref.shape[0], rest, 0)
    sum_ref[...] = acc_ref[...].astype(BF16)


def merge_kernel(me_ref, pick_ref, ret_ref, *out_refs):
    nz = len(out_refs)
    for s, out_ref in enumerate(out_refs):
        to = lax.rem(me_ref[0] + s, nz)
        rows = jnp.concatenate([ret_ref[u, to] for u in range(ret_ref.shape[0])], axis=0)
        out_ref[...] = dot(pick_ref[to], rows, NN).astype(BF16)


def finish_kernel(*refs, cols):
    *ins, att_ref, grad_ref = refs
    many = len(ins) // 2
    lane = lax.broadcasted_iota(jnp.int32, (1, 256), 1)
    low = (lane < cols).astype(BF16)
    high = (lane >= cols - 128).astype(BF16)
    att, grad = 0.0, 0.0
    for x_ref, w_ref in zip(ins[:many], ins[many:]):
        grad = grad + dot(x_ref[:, 0:256] * low, w_ref[:, 0:256], NT)
        att = att + dot(x_ref[:, 128:384] * high, w_ref[:, 128:384], NT)
    att_ref[...] = att.astype(BF16)
    grad_ref[...] = grad.astype(BF16)


def call(kernel, out_shape, ins, outs, scratch=(), mib=1):
    spaces = {"s": pltpu.SMEM, "v": pltpu.VMEM, "a": pltpu.HBM}
    out_specs = [pl.BlockSpec(memory_space=spaces[i]) for i in outs]
    return pl.pallas_call(
        kernel,
        out_shape=out_shape,
        in_specs=[pl.BlockSpec(memory_space=spaces[i]) for i in ins],
        out_specs=out_specs if len(outs) > 1 else out_specs[0],
        scratch_shapes=list(scratch),
        compiler_params=pltpu.CompilerParams(vmem_limit_bytes=mib * 1024 * 1024),
    )


def mp_hop(value, s):
    many = lax.axis_size("mp")
    return lax.ppermute(value, "mp", [(i, (i + s) % many) for i in range(many)])


def body(frames, keyframes, query_states, w_query, w_key, w_value, w_out, out_grad):
    owners = lax.axis_size("frames")
    shards = lax.axis_size("mp")
    me, shard = lax.axis_index("frames"), lax.axis_index("mp")
    fr_count, tok, width = frames.shape
    quests, keys = keyframes.shape
    nq = query_states.shape[1]
    hid = query_states.shape[2]
    cols = w_key.shape[1]
    heads = cols // HEAD_DIM
    scale = HEAD_DIM ** (-0.5)
    count = quests * keys
    cap = max(2, count // owners)
    group = 4

    queries = jnp.dot(query_states.reshape(quests * nq, hid), w_query, preferred_element_type=F32)
    d_mixed = lax.dot_general(out_grad.reshape(quests * nq, hid), w_out, NT, preferred_element_type=F32)
    local = jnp.concatenate([queries.astype(BF16) * scale, d_mixed.astype(BF16)], axis=1)
    picks = keyframes.reshape(-1)
    owner = picks >> (fr_count.bit_length() - 1)
    position = jnp.arange(count)
    same = owner[:, None] == owner[None, :]
    rank = jnp.sum(jnp.logical_and(same, position[None, :] < position[:, None]), axis=1)
    code = (picks & (fr_count - 1)) + fr_count * (position // keys) + 1
    slot = owner * cap + rank
    requests = jnp.sum(
        jnp.where(slot[None, :] == jnp.arange(owners * cap)[:, None], code[None, :], 0), axis=1
    ).astype(jnp.int32)
    asked = jnp.where(requests > 0, (requests - 1) >> (fr_count.bit_length() - 1), -1)
    quest_of = jnp.broadcast_to(asked.reshape(owners, cap).T[:, :, None], (cap, owners, 128))
    put = jnp.arange(quests * nq)[:, None]
    take = jnp.arange(owners * cap * nq)[None, :]
    pick_sum = jnp.logical_and(put // nq == jnp.repeat(asked, nq)[None, :], put % nq == take % nq).astype(BF16)

    w_both = jnp.concatenate([w_key, w_value], axis=1)
    bank = jnp.dot(frames.reshape(fr_count * tok, width), w_both, preferred_element_type=F32).astype(BF16)
    flat, line = planes()
    nx, nz, nc = AXES
    mine = jnp.concatenate([local] + [hop(local, dx=s) for s in range(1, nx)], axis=0)
    passed = requests.reshape(nx, nz, nc, cap).swapaxes(0, 1).reshape(nz, nx * nc * cap)
    passed = lax.all_to_all(passed, "frames", 0, 0, axis_index_groups=line, tiled=True)
    mine, passed, bank = lax.optimization_barrier((mine, passed, bank))
    incoming = passed.reshape(nz, nx * nc, cap).swapaxes(0, 1).reshape(nx * nc, nz * cap)
    incoming = lax.all_to_all(incoming, "frames", 0, 0, axis_index_groups=flat, tiled=True)
    incoming = incoming.reshape(nx * nc, nz, cap).swapaxes(0, 1).reshape(-1)
    ways = [(mine, mine)]
    ways.append((hop(ways[-1][0], dz=1), hop(ways[-1][1], dz=-1)))
    ways[-1], incoming = lax.optimization_barrier((ways[-1], incoming))
    ints = lambda *shape: jax.ShapeDtypeStruct(shape, jnp.int32)
    order, sizes, at = call(
        functools.partial(plan_kernel, cap=cap, quests=quests, nq=nq, tok=tok, frames_here=fr_count),
        (ints(owners), ints(2), ints(2 * owners * cap)),
        "ss",
        "sss",
    )(incoming, me.astype(jnp.int32).reshape(1))
    ways.append((hop(ways[-1][0], dz=1), hop(ways[-1][1], dz=-1)))
    ways[-1], order, sizes, at, quest_of = lax.optimization_barrier((ways[-1], order, sizes, at, quest_of))
    ways.append((hop(ways[-1][0], dz=1), hop(ways[-1][1], dz=-1)))
    half = mine.shape[0] // 2
    pieces = [mine] + [way for pair in ways[1:] for way in pair]
    pieces += [hop(ways[-1][0][:half], dz=1), hop(ways[-1][1][half:], dz=-1)]
    pieces = [p for piece in pieces for p in (piece, hop(piece, dc=1))]

    dims = dict(cap=cap, nq=nq, tok=tok, heads=heads, group=group)
    held = (owners * cap * nq, 2 * cols)
    stat_shape = jax.ShapeDtypeStruct((owners, 8, 128), F32)
    rows = jax.ShapeDtypeStruct((owners * quests * nq, 2 * cols), BF16)
    stats, rows = call(
        functools.partial(stats_kernel, **dims),
        (stat_shape, rows),
        "sssv" + "a" * len(pieces),
        "vv",
        [pltpu.SemaphoreType.DMA((len(pieces),))],
        4,
    )(order, sizes, at, bank, *pieces)
    stats = lax.all_to_all(stats, "frames", split_axis=0, concat_axis=0, tiled=True)
    stats = call(functools.partial(combine_kernel, cap=cap, quests=quests), stat_shape, "vv", "v")(quest_of, stats)
    stats = lax.all_to_all(stats, "frames", split_axis=0, concat_axis=0, tiled=True)
    partial, sums = call(
        functools.partial(main_kernel, scale=scale, **dims),
        (jax.ShapeDtypeStruct(held, BF16), jax.ShapeDtypeStruct((fr_count * tok, 2 * cols), BF16)),
        "sssvvv",
        "vv",
        [pltpu.VMEM((fr_count * tok, 2 * cols), F32)],
        8,
    )(order, sizes, at, bank, stats, rows)
    partial = lax.all_to_all(
        partial.reshape(nx * nc, nz * cap * nq, 2 * cols), "frames", 0, 0, axis_index_groups=flat, tiled=True
    ).reshape(nx * nc, nz, cap * nq, 2 * cols)
    asked = jnp.where(passed > 0, (passed - 1) >> (fr_count.bit_length() - 1), -1)
    put = jnp.arange(quests * nq)[None, :, None]
    take = jnp.arange(nx * nc * cap * nq)[None, None, :]
    asked = jnp.repeat(asked.reshape(nz, 1, nx * nc * cap), nq, axis=2)
    pick_sum = jnp.logical_and(put // nq == asked, put % nq == take % nq).astype(BF16)

    w_q_out = jnp.concatenate([w_query, w_out.T], axis=1)
    own = [(shard + s) % shards for s in range(shards)]
    part = hid // shards
    slab = width // shards
    terms = [
        lax.dot_general(
            sums, lax.dynamic_slice_in_dim(w_both, own[s] * slab, slab, 0), NT, preferred_element_type=F32
        )
        for s in range(shards)
    ]
    frame_grad = terms[0]
    for s in range(1, shards):
        frame_grad = frame_grad + mp_hop(terms[s].astype(BF16), s).astype(F32)

    frame_grad = frame_grad.astype(BF16).reshape(fr_count, tok, slab)
    partial, w_q_out, pick_sum = lax.optimization_barrier((partial, w_q_out, pick_sum))
    mine_shape = jax.ShapeDtypeStruct((quests * nq, 2 * cols), BF16)
    merged = call(merge_kernel, (mine_shape,) * nz, "svv", "v" * nz, mib=4)(
        lax.rem(lax.div(me, nc), nz).astype(jnp.int32).reshape(1), pick_sum, partial
    )
    parts = [merged[0]] + [hop(merged[s], dz=s) for s in range(1, nz)]
    parts, frame_grad = lax.optimization_barrier((parts, frame_grad))
    blocks = call(
        functools.partial(project_kernel, cols=cols),
        jax.ShapeDtypeStruct((shards, 2 * quests * nq, part), BF16),
        "v" * (nz + 1),
        "v",
        mib=2,
    )(*parts, w_q_out)
    blocks = lax.all_to_all(blocks, "mp", 0, 0, tiled=True)
    out = jax.ShapeDtypeStruct((quests * nq, part), BF16)
    attended, query_grad = call(add_kernel, (out, out), "v", "vv")(blocks)
    return attended.reshape(quests, nq, part), query_grad.reshape(quests, nq, part), frame_grad


def solution(mesh):
    placed = (
        P("frames", None, None),
        P("frames", None),
        P("frames", None, None),
        P(None, "mp"),
        P(None, "mp"),
        P(None, "mp"),
        P("mp", None),
        P("frames", None, None),
    )
    return jax.shard_map(
        body,
        mesh=mesh,
        in_specs=placed,
        out_specs=(P("frames", None, "mp"), P("frames", None, "mp"), P("frames", None, "mp")),
        check_vma=False,
    )
```
